32 devices in a mesh: query: 4 (over y, x), cluster: 8 (over z, core).
Axes of the slice: x: 2, y: 2, z: 4, core: 2. Of those that a mesh axis runs over, the one named last changes fastest.
Arguments:
- queries: bfloat16 [1024, 512], P(('query', 'cluster')), may hold values from -68 to 68
- centroids: bfloat16 [64, 512], P('cluster'), may hold values from -6 to 6
- leaves: bfloat16 [64, 1024, 512], P('cluster'), may hold values from -5 to 5
- beam: int32 [1024, 8], P('query'), may hold values from 0 to 63, all different within a row; in each aligned block of 256 rows (0 to 255, 256 to 511, ...) at most 64 rows name the same one
Outputs:
- readout: bfloat16 [1024, 512], P(('query', 'cluster'))
- beam_logprob: float32 [1024, 8], P(('query', 'cluster'))
The draws below stay inside these ranges and needn't reach their ends.
Inputs may be any that keep to these rules, and one draw needn't show every extreme that they name: `beam`: each row names 8 different clusters. In each aligned block of 256 rows (the queries of one index of query) no cluster is named by more than 64 rows, a bound that some block reaches.
All inputs are finite; a program needn't handle non-finite values.
Results may differ from the reference program's by a relative error of at most 0.0028.
Values may be sent and summed in bfloat16 or wider, within the bound.
A program may use at most 128 MiB of HBM per device.

```python
import math
import jax
import jax.numpy as jnp
import numpy as np
from jax import lax

D = 512
LEAF = 1024
TOP = 8
Q_DEV = 256
NCL = 64
NQ = 1024
CAP = 64


def draw_queries(key, part):
    second_key = jax.random.fold_in(jax.random.fold_in(key, 11), 1)
    base = jnp.clip(jax.random.normal(second_key, (NQ, D)), -5.0, 5.0)
    return (2.5 * base).astype(jnp.bfloat16)


def draw_leaves(key, part):
    first_key = jax.random.fold_in(jax.random.fold_in(key, 23), 0)
    base = jnp.clip(jax.random.normal(first_key, (NCL, LEAF, D)), -5.0, 5.0)
    return base.astype(jnp.bfloat16)


def level_of(rng, dims, pieces, least, largest):
    level = 1.0
    for dim, parts in pieces:
        heights = jax.random.uniform(jax.random.fold_in(jax.random.fold_in(rng, 6), dim), (parts,), jnp.float32, least / len(pieces), largest / len(pieces))
        level = level * jnp.repeat(jnp.exp(heights), dims[dim] // parts).reshape((-1,) + (1,) * (len(dims) - 1 - dim))
    return level


def assign_block(rng, own, number, rows, count, top, reach, slope):
    ranking = jax.random.permutation(rng, count)
    crowded, ordinary = load_shares(count, rows * top, reach, slope, True), load_shares(count, rows * top, reach, slope, False)
    places = jnp.arange(count)

    def named(tallies, offset_by):
        used = int((tallies > 0).sum())
        fixed = max(1, used // 4)
        shifted = fixed + (places - fixed + offset_by * (used - fixed)) % max(1, count - fixed)
        return jnp.zeros((count,), jnp.int32).at[ranking[jnp.where(places < fixed, places, shifted)]].set(jnp.asarray(tallies, jnp.int32))

    tallies = jnp.where(number % 4 == 0, named(crowded, number // 4), named(ordinary, number - number // 4 - 1))
    mixed = jax.random.permutation(jax.random.fold_in(own, 3), count)
    source_of, sink = mixed[0:count // 2 * 2:2], mixed[1:count // 2 * 2:2]
    room = jnp.minimum(tallies[source_of] - 1, reach - tallies[sink]) // 2
    room = jnp.where((source_of == ranking[0]) | (sink == ranking[0]) | (tallies[sink] == 0), 0, jnp.maximum(room, 0))
    shifted = jax.random.randint(jax.random.fold_in(own, 4), (count // 2,), 0, 1 << 20) % (room + 1)
    tallies = tallies.at[source_of].add(-shifted).at[sink].add(shifted)
    members = jnp.searchsorted(jnp.cumsum(tallies), jnp.arange(rows * top), side="right").astype(jnp.int32)
    listing = members.reshape(top, rows).T
    listing = listing[jax.random.permutation(jax.random.fold_in(own, 1), rows)]
    offset_by = jax.random.randint(jax.random.fold_in(own, 2), (rows, 1), 0, top)
    return jnp.take_along_axis(listing, (jnp.arange(top)[None, :] + offset_by) % top, axis=1)


def load_shares(number_of, total, bound, slope, full):
    weights = [(1 << 20) // math.isqrt(grade ** slope) + 1 for grade in range(1, number_of + 1)]
    largest = bound if full else min(bound, max(-(-total // number_of), total * weights[0] // sum(weights)))
    least = 1 if total - largest >= number_of - 1 else 0
    counts, surplus = [largest] + [least] * (number_of - 1), total - largest - least * (number_of - 1)
    while surplus > 0:
        candidates = [i for i in range(1, number_of) if counts[i] < largest] or [i for i in range(1, number_of) if counts[i] < bound]
        mass, left = sum([weights[i] for i in candidates]), surplus
        for i in candidates:
            more = min(bound - counts[i], max(1, left * weights[i] // mass), surplus)
            counts[i] = counts[i] + more
            surplus = surplus - more
    return np.array(counts)


def gaussian(rng, dims, deviation, most, shards=(), held_as=jnp.bfloat16):
    factor_of = level_of(rng, dims, shards, -0.22, 0.18) if shards else 1.0
    array = jax.random.normal(rng, dims, jnp.float32) * deviation * factor_of
    return jnp.minimum(jnp.maximum(array, -most), most).astype(held_as)


def setup_inputs(seed: int = 0) -> dict:
    arg_keys = jax.random.split(jax.random.key(seed), 5)
    queries = draw_queries(jax.random.fold_in(arg_keys[4], 71), 0)
    centroids = gaussian(arg_keys[1], (NCL, D), 1.0, 6.0, ((0, 8),))
    leaves = draw_leaves(jax.random.fold_in(arg_keys[4], 71), 0)
    beam_keys = jax.random.split(jax.random.fold_in(arg_keys[3], 1), NQ // Q_DEV)
    beam_turns = jax.random.permutation(jax.random.fold_in(arg_keys[3], 3), NQ // Q_DEV)
    beam = jax.vmap(lambda own, number: assign_block(jax.random.fold_in(arg_keys[3], 2), own, number, Q_DEV, NCL, TOP, CAP, 2))(beam_keys, beam_turns).reshape((NQ, TOP))
    return dict(queries=queries, centroids=centroids, leaves=leaves, beam=beam)


def reference(queries, centroids, leaves, beam):
    score_scale = 1.0 / math.sqrt(D)
    cscore = jnp.dot(queries, centroids.T, preferred_element_type=jnp.float32) * score_scale
    cmax = lax.optimization_barrier(jnp.max(cscore, axis=1))
    lse = cmax + jnp.log(lax.optimization_barrier(jnp.sum(jnp.exp(cscore - cmax[:, None]), axis=1)))
    beam_score = jnp.take_along_axis(cscore, beam, axis=1)
    beam_logprob = beam_score - lse[:, None]

    def one_block(packed):
        query_block, beam_block, score_block = packed
        gathered = leaves[beam_block].astype(jnp.float32)
        logits = jnp.einsum('qd,qkjd->qkj', query_block.astype(jnp.float32), gathered) * score_scale
        logits = logits + score_block[:, :, None]
        block_max = lax.optimization_barrier(jnp.max(logits, axis=2))
        weights = jnp.exp(logits - block_max[:, :, None])
        totals = lax.optimization_barrier(jnp.sum(weights, axis=2))
        rounded = weights.astype(jnp.bfloat16).astype(jnp.float32)
        accum = jnp.einsum('qkj,qkjd->qkd', rounded, gathered)
        overall = lax.optimization_barrier(jnp.max(block_max, axis=1))
        factor = jnp.exp(block_max - overall[:, None])
        numer = lax.optimization_barrier(jnp.sum(factor[:, :, None] * accum, axis=1))
        denom = lax.optimization_barrier(jnp.sum(factor * totals, axis=1))
        return (numer / denom[:, None]).astype(jnp.bfloat16)
    block_rows = 8
    packed = (queries.reshape(NQ // block_rows, block_rows, D), beam.reshape(NQ // block_rows, block_rows, TOP), beam_score.reshape(NQ // block_rows, block_rows, TOP))
    readout = lax.map(one_block, packed).reshape(NQ, D)
    return (readout, beam_logprob)
```

```python
import functools
import math

import jax
import jax.numpy as jnp
from jax import lax
from jax.experimental import pallas as pl
from jax.experimental.pallas import tpu as pltpu
from jax.sharding import PartitionSpec as P

floor_value = -1e30


def merged_2(part, axis, combine):
    gathered = jax.tree.map(lambda a: lax.all_gather(a, axis), part)

    def take(source):
        return jax.tree.map(lambda a: lax.dynamic_index_in_dim(a, source, 0, False), gathered)

    return lax.fori_loop(
        1, lax.axis_size(axis), lambda source, state: combine(state, take(source)), take(0)
    )


def combine_states(first, second):
    cmax_one, csum_one, beam_one, lmax_one, lsum_one, accum_one = first
    cmax_two, csum_two, beam_two, lmax_two, lsum_two, accum_two = second
    cmax_new = jnp.maximum(cmax_one, cmax_two)
    csum_new = csum_one * jnp.exp(cmax_one - cmax_new) + csum_two * jnp.exp(cmax_two - cmax_new)
    lmax_new = jnp.maximum(lmax_one, lmax_two)
    factor_one = jnp.exp(lmax_one - lmax_new)
    factor_two = jnp.exp(lmax_two - lmax_new)
    lsum_new = lsum_one * factor_one + lsum_two * factor_two
    accum_new = accum_one * factor_one[:, None] + accum_two * factor_two[:, None]
    return (cmax_new, csum_new, beam_one + beam_two, lmax_new, lsum_new, accum_new)


def per_device(queries, centroids, leaves, beam):
    groups = lax.axis_size("cluster")
    query_block = lax.all_gather(queries, "cluster", axis=0, tiled=True)
    query_count, model_width = query_block.shape
    cluster_count, leaf_count, unused_width = leaves.shape
    beam_width = beam.shape[1]
    score_scale = 1.0 / math.sqrt(model_width)
    first_cluster = lax.axis_index("cluster") * cluster_count
    cscore = jnp.dot(query_block, centroids.T, preferred_element_type=jnp.float32) * score_scale
    cmax_part = jnp.max(cscore, axis=1)
    csum_part = jnp.sum(jnp.exp(cscore - cmax_part[:, None]), axis=1)
    owned = first_cluster + jnp.arange(cluster_count, dtype=jnp.int32)
    matches = beam[:, :, None] == owned[None, None, :]
    beam_part = jnp.sum(jnp.where(matches, cscore[:, None, :], 0.0), axis=2)
    membership = jnp.any(matches, axis=1).astype(jnp.int32)
    slot_index = jnp.cumsum(membership, axis=0) - 1
    capacity = max(4, 2 * query_count * beam_width // (cluster_count * groups))
    positions = jnp.arange(capacity, dtype=jnp.int32)
    dispatch = (membership.T[:, None, :] == 1) & (
        slot_index.T[:, None, :] == positions[None, :, None]
    )
    picked = jnp.einsum(
        "csq,qd->csd",
        dispatch.astype(jnp.bfloat16),
        query_block,
        preferred_element_type=jnp.float32,
    ).astype(jnp.bfloat16)
    slot_centroid = jnp.sum(jnp.where(dispatch, cscore.T[:, None, :], 0.0), axis=2)
    logits = (
        jnp.einsum("csd,cjd->csj", picked, leaves, preferred_element_type=jnp.float32) * score_scale
    )
    logits = logits + slot_centroid[:, :, None]
    slot_max = jnp.max(logits, axis=2)
    weights = jnp.exp(logits - slot_max[:, :, None])
    slot_sum = jnp.sum(weights, axis=2)
    slot_accum = jnp.einsum(
        "csj,cjd->csd", weights.astype(jnp.bfloat16), leaves, preferred_element_type=jnp.float32
    )
    slot_total = cluster_count * capacity
    dispatch_flat = dispatch.reshape(slot_total, query_count)
    slot_max_flat = slot_max.reshape(slot_total)
    masked_max = jnp.where(dispatch_flat, slot_max_flat[:, None], floor_value)
    lmax_part = jnp.max(masked_max, axis=0)
    exponent = jnp.where(dispatch_flat, slot_max_flat[:, None] - lmax_part[None, :], 0.0)
    factors = jnp.where(dispatch_flat, jnp.exp(exponent), 0.0)
    lsum_part = jnp.sum(factors * slot_sum.reshape(slot_total)[:, None], axis=0)
    accum_part = jnp.dot(
        factors.T,
        slot_accum.reshape(slot_total, model_width),
        precision=lax.Precision.HIGHEST,
        preferred_element_type=jnp.float32,
    )
    state = (cmax_part, csum_part, beam_part, lmax_part, lsum_part, accum_part)
    row_count = query_count // groups
    merged = merged_2(state, "cluster", combine_states)
    row_start = lax.axis_index("cluster") * row_count
    own = tuple((lax.dynamic_slice_in_dim(member, row_start, row_count, 0) for member in merged))
    cmax_own, csum_own, beam_own, lmax_own, lsum_own, accum_own = own
    lse = cmax_own + jnp.log(csum_own)
    beam_logprob = beam_own - lse[:, None]
    readout = (accum_own / lsum_own[:, None]).astype(jnp.bfloat16)
    return (readout, beam_logprob)


MESH = pl.DeviceIdType.MESH
CODE_MAX = 32767.0
LANES = 128


def fused_kernel(
    groups,
    q_ref,
    cent_ref,
    leaves_ref,
    beam_ref,
    readout_ref,
    logprob_ref,
    block,
    leaf_buf,
    cscore_send,
    cscore_recv,
    stat_send,
    stat_recv,
    code_send,
    code_recv,
    accum,
    leaf_sem,
    own_sem,
    q_send_sem,
    q_recv_sem,
    cscore_send_sem,
    cscore_recv_sem,
    stat_send_sem,
    stat_recv_sem,
    code_send_sem,
    code_recv_sem,
):
    rows, width = q_ref.shape
    clusters = cent_ref.shape[0]
    total = groups * rows
    beam_width = beam_ref.shape[1]
    chips = groups // 2
    score_scale = 1.0 / math.sqrt(width)
    me = lax.axis_index("cluster")
    chip, core = me // 2, me % 2
    sibling = chip * 2 + (1 - core)
    first = me * clusters

    def peer_at(offset, side):
        return lax.rem(chip + offset, chips) * 2 + side

    peers = [peer_at(o, s) for o in range(1, chips) for s in (core, 1 - core)] + [sibling]

    leaf_copies = [
        pltpu.make_async_copy(leaves_ref.at[c], leaf_buf.at[c], leaf_sem.at[c])
        for c in range(clusters)
    ]
    for copy in leaf_copies:
        copy.start()
    own_copy = pltpu.make_async_copy(q_ref, block.at[me], own_sem)
    own_copy.start()

    barrier = pltpu.get_barrier_semaphore()
    for peer in peers:
        pl.semaphore_signal(barrier, inc=1, device_id={"cluster": peer}, device_id_type=MESH)
    pl.semaphore_wait(barrier, len(peers))

    def push(src, dst, send_sem, recv_sem, peer):
        return pltpu.make_async_remote_copy(
            src_ref=src,
            dst_ref=dst,
            send_sem=send_sem,
            recv_sem=recv_sem,
            device_id={"cluster": peer},
            device_id_type=MESH,
        )

    sends = []
    for number, offset in enumerate(range(1, chips)):
        peer = peer_at(offset, core)
        sends.append(push(q_ref, block.at[me], q_send_sem.at[number], q_recv_sem.at[me], peer))
    sends.append(push(q_ref, block.at[me], q_send_sem.at[chips - 1], q_recv_sem.at[me], sibling))
    for copy in sends:
        copy.start()

    def arrival(origin):
        return push(block.at[origin], block.at[origin], q_send_sem.at[0], q_recv_sem.at[origin], sibling)

    for offset in range(1, chips):
        origin = peer_at(chips - offset, core)
        arrival(origin).wait_recv()
        relay = push(
            block.at[origin],
            block.at[origin],
            q_send_sem.at[chips - 1 + offset],
            q_recv_sem.at[origin],
            sibling,
        )
        relay.start()
        sends.append(relay)
    arrival(sibling).wait_recv()
    for offset in range(1, chips):
        arrival(peer_at(chips - offset, 1 - core)).wait_recv()
    own_copy.wait()

    queries = block[...].reshape(total, width)
    lane = lax.broadcasted_iota(jnp.int32, (total, LANES), 1)
    cent = jnp.concatenate(
        [cent_ref[...], jnp.zeros((LANES - clusters, width), cent_ref.dtype)], axis=0
    )
    nt = (((1,), (1,)), ((), ()))
    cscore = lax.dot_general(queries, cent, nt, preferred_element_type=jnp.float32) * score_scale
    cscore_send[...] = cscore.reshape(groups, rows, LANES)

    cscore_copies = []
    for number, peer in enumerate(peers):
        cscore_copies.append(
            push(
                cscore_send.at[peer],
                cscore_recv.at[me],
                cscore_send_sem.at[number],
                cscore_recv_sem.at[me],
                peer,
            )
        )
    for copy in cscore_copies:
        copy.start()

    beams = beam_ref[...]
    top = jnp.full((total, 1), floor_value, jnp.float32)
    denom = jnp.zeros((total, 1), jnp.float32)

    def scores(c):
        leaf_copies[c].wait()
        return lax.dot_general(queries, leaf_buf[c], nt, preferred_element_type=jnp.float32)

    current = scores(0)
    for c in range(clusters):
        upcoming = scores(c + 1) if c + 1 < clusters else None
        member = jnp.max((beams == first + c).astype(jnp.float32), axis=1, keepdims=True) > 0.0
        centroid = jnp.sum(jnp.where(lane == c, cscore, 0.0), axis=1, keepdims=True)
        peak = jnp.max(current, axis=1, keepdims=True)
        weights = jnp.exp((current - peak) * score_scale)
        mass = jnp.sum(weights, axis=1, keepdims=True)
        summed = jnp.dot(
            weights.astype(jnp.bfloat16), leaf_buf[c], preferred_element_type=jnp.float32
        )
        level = jnp.where(member, peak * score_scale + centroid, floor_value)
        raised = jnp.maximum(top, level)
        keep = jnp.exp(top - raised)
        gain = jnp.where(member, jnp.exp(level - raised), 0.0)
        denom = denom * keep + mass * gain
        if c == 0:
            accum[...] = summed * gain
        else:
            accum[...] = accum[...] * keep + summed * gain
        top = raised
        current = upcoming

    held = accum[...]
    largest = jnp.maximum(jnp.max(jnp.abs(held), axis=1, keepdims=True), 1e-30)
    coded = jnp.round(held * (CODE_MAX / largest)).astype(jnp.int32).astype(jnp.int16)
    code_send[...] = coded.reshape(groups, rows, width)
    stats = jnp.where(lane == 0, top, jnp.where(lane == 1, denom, largest * (1.0 / CODE_MAX)))
    flipped = stats.T
    for g in range(groups):
        stat_send[g, :, 0:rows] = flipped[0:8, g * rows : (g + 1) * rows]

    result_copies = []
    for number, peer in enumerate(peers):
        result_copies.append(
            push(
                stat_send.at[peer],
                stat_recv.at[me],
                stat_send_sem.at[number],
                stat_recv_sem.at[me],
                peer,
            )
        )
        result_copies.append(
            push(
                code_send.at[peer],
                code_recv.at[me],
                code_send_sem.at[number],
                code_recv_sem.at[me],
                peer,
            )
        )
    for copy in result_copies:
        copy.start()

    for number, peer in enumerate(peers):
        push(
            cscore_send.at[peer],
            cscore_recv.at[peer],
            cscore_send_sem.at[number],
            cscore_recv_sem.at[peer],
            peer,
        ).wait_recv()
    cscore_recv[me] = cscore_send[me]
    all_scores = [cscore_recv[g] for g in range(groups)]
    small_lane = lax.broadcasted_iota(jnp.int32, (rows, LANES), 1)
    real = small_lane < clusters
    cmax = functools.reduce(jnp.maximum, [jnp.where(real, s, floor_value) for s in all_scores])
    cmax = jnp.max(cmax, axis=1, keepdims=True)
    csum = sum(jnp.where(real, jnp.exp(s - cmax), 0.0) for s in all_scores)
    lse = cmax + jnp.log(jnp.sum(csum, axis=1, keepdims=True))
    own_beams = beam_ref[pl.ds(pl.multiple_of(me * rows, rows), rows), :]
    picks = jnp.zeros((rows, LANES), jnp.float32)
    for k in range(beam_width):
        wanted = own_beams[:, k : k + 1]
        found = sum(
            jnp.where(real & (wanted == small_lane + g * clusters), s, 0.0)
            for g, s in enumerate(all_scores)
        )
        picks = jnp.where(small_lane == k, jnp.sum(found, axis=1, keepdims=True), picks)
    logprob_ref[...] = (picks - lse)[:, 0:beam_width]

    for number, peer in enumerate(peers):
        push(
            stat_send.at[peer],
            stat_recv.at[peer],
            stat_send_sem.at[number],
            stat_recv_sem.at[peer],
            peer,
        ).wait_recv()
    stat_recv[me] = stat_send[me]
    code_recv[me] = code_send[me]
    tops = stat_recv[:, 0, :]
    overall = jnp.max(tops, axis=0, keepdims=True)
    factors = jnp.exp(tops - overall)
    whole = jnp.sum(factors * stat_recv[:, 1, :], axis=0, keepdims=True)
    shares = factors * stat_recv[:, 2, :] / whole
    shares = jnp.concatenate(
        [shares, jnp.zeros((LANES - groups, LANES), jnp.float32)], axis=0
    ).T[0:rows]

    for number, peer in enumerate(peers):
        push(
            code_send.at[peer],
            code_recv.at[peer],
            code_send_sem.at[number],
            code_recv_sem.at[peer],
            peer,
        ).wait_recv()
    merged = jnp.zeros((rows, width), jnp.float32)
    for g in range(groups):
        merged = merged + code_recv[g].astype(jnp.int32).astype(jnp.float32) * shares[:, g : g + 1]
    readout_ref[...] = merged.astype(jnp.bfloat16)

    for copy in sends + cscore_copies + result_copies:
        copy.wait_send()


def fused(queries, centroids, leaves, beam):
    groups = lax.axis_size("cluster")
    rows, width = queries.shape
    clusters = centroids.shape[0]
    if rows % 16 or groups % 2 or groups > 16 or rows > LANES:
        return per_device(queries, centroids, leaves, beam)
    vmem = pl.BlockSpec(memory_space=pltpu.VMEM)
    dma = pltpu.SemaphoreType.DMA
    peers = groups - 1
    return pl.pallas_call(
        functools.partial(fused_kernel, groups),
        out_shape=(
            jax.ShapeDtypeStruct((rows, width), jnp.bfloat16),
            jax.ShapeDtypeStruct((rows, beam.shape[1]), jnp.float32),
        ),
        in_specs=[vmem, vmem, pl.BlockSpec(memory_space=pl.ANY), vmem],
        out_specs=(vmem, vmem),
        scratch_shapes=[
            pltpu.VMEM((groups, rows, width), jnp.bfloat16),
            pltpu.VMEM(leaves.shape, jnp.bfloat16),
            pltpu.VMEM((groups, rows, LANES), jnp.float32),
            pltpu.VMEM((groups, rows, LANES), jnp.float32),
            pltpu.VMEM((groups, 8, LANES), jnp.float32),
            pltpu.VMEM((groups, 8, LANES), jnp.float32),
            pltpu.VMEM((groups, rows, width), jnp.int16),
            pltpu.VMEM((groups, rows, width), jnp.int16),
            pltpu.VMEM((groups * rows, width), jnp.float32),
            dma((clusters,)),
            dma,
            dma((groups,)),
            dma((groups,)),
            dma((peers,)),
            dma((groups,)),
            dma((peers,)),
            dma((groups,)),
            dma((peers,)),
            dma((groups,)),
        ],
        compiler_params=pltpu.CompilerParams(
            collective_id=0, has_side_effects=True, vmem_limit_bytes=48 * 1024 * 1024
        ),
    )(queries, centroids, leaves, beam)


def solution(mesh):
    return jax.shard_map(
        fused,
        mesh=mesh,
        in_specs=(
            P(("query", "cluster"), None),
            P("cluster", None),
            P("cluster", None, None),
            P("query", None),
        ),
        out_specs=(P(("query", "cluster"), None), P(("query", "cluster"), None)),
        check_vma=False,
    )
```

```python
import functools
import math

import jax
import jax.numpy as jnp
from jax import lax
from jax.experimental import pallas as pl
from jax.experimental.pallas import tpu as pltpu
from jax.sharding import PartitionSpec as P

floor_value = -1e30


def merged_2(part, axis, combine):
    gathered = jax.tree.map(lambda a: lax.all_gather(a, axis), part)

    def take(source):
        return jax.tree.map(lambda a: lax.dynamic_index_in_dim(a, source, 0, False), gathered)

    return lax.fori_loop(
        1, lax.axis_size(axis), lambda source, state: combine(state, take(source)), take(0)
    )


def combine_states(first, second):
    cmax_one, csum_one, beam_one, lmax_one, lsum_one, accum_one = first
    cmax_two, csum_two, beam_two, lmax_two, lsum_two, accum_two = second
    cmax_new = jnp.maximum(cmax_one, cmax_two)
    csum_new = csum_one * jnp.exp(cmax_one - cmax_new) + csum_two * jnp.exp(cmax_two - cmax_new)
    lmax_new = jnp.maximum(lmax_one, lmax_two)
    factor_one = jnp.exp(lmax_one - lmax_new)
    factor_two = jnp.exp(lmax_two - lmax_new)
    lsum_new = lsum_one * factor_one + lsum_two * factor_two
    accum_new = accum_one * factor_one[:, None] + accum_two * factor_two[:, None]
    return (cmax_new, csum_new, beam_one + beam_two, lmax_new, lsum_new, accum_new)


def per_device(queries, centroids, leaves, beam):
    groups = lax.axis_size("cluster")
    query_block = lax.all_gather(queries, "cluster", axis=0, tiled=True)
    query_count, model_width = query_block.shape
    cluster_count, leaf_count, unused_width = leaves.shape
    beam_width = beam.shape[1]
    score_scale = 1.0 / math.sqrt(model_width)
    first_cluster = lax.axis_index("cluster") * cluster_count
    cscore = jnp.dot(query_block, centroids.T, preferred_element_type=jnp.float32) * score_scale
    cmax_part = jnp.max(cscore, axis=1)
    csum_part = jnp.sum(jnp.exp(cscore - cmax_part[:, None]), axis=1)
    owned = first_cluster + jnp.arange(cluster_count, dtype=jnp.int32)
    matches = beam[:, :, None] == owned[None, None, :]
    beam_part = jnp.sum(jnp.where(matches, cscore[:, None, :], 0.0), axis=2)
    membership = jnp.any(matches, axis=1).astype(jnp.int32)
    slot_index = jnp.cumsum(membership, axis=0) - 1
    capacity = max(4, 2 * query_count * beam_width // (cluster_count * groups))
    positions = jnp.arange(capacity, dtype=jnp.int32)
    dispatch = (membership.T[:, None, :] == 1) & (
        slot_index.T[:, None, :] == positions[None, :, None]
    )
    picked = jnp.einsum(
        "csq,qd->csd",
        dispatch.astype(jnp.bfloat16),
        query_block,
        preferred_element_type=jnp.float32,
    ).astype(jnp.bfloat16)
    slot_centroid = jnp.sum(jnp.where(dispatch, cscore.T[:, None, :], 0.0), axis=2)
    logits = (
        jnp.einsum("csd,cjd->csj", picked, leaves, preferred_element_type=jnp.float32) * score_scale
    )
    logits = logits + slot_centroid[:, :, None]
    slot_max = jnp.max(logits, axis=2)
    weights = jnp.exp(logits - slot_max[:, :, None])
    slot_sum = jnp.sum(weights, axis=2)
    slot_accum = jnp.einsum(
        "csj,cjd->csd", weights.astype(jnp.bfloat16), leaves, preferred_element_type=jnp.float32
    )
    slot_total = cluster_count * capacity
    dispatch_flat = dispatch.reshape(slot_total, query_count)
    slot_max_flat = slot_max.reshape(slot_total)
    masked_max = jnp.where(dispatch_flat, slot_max_flat[:, None], floor_value)
    lmax_part = jnp.max(masked_max, axis=0)
    exponent = jnp.where(dispatch_flat, slot_max_flat[:, None] - lmax_part[None, :], 0.0)
    factors = jnp.where(dispatch_flat, jnp.exp(exponent), 0.0)
    lsum_part = jnp.sum(factors * slot_sum.reshape(slot_total)[:, None], axis=0)
    accum_part = jnp.dot(
        factors.T,
        slot_accum.reshape(slot_total, model_width),
        precision=lax.Precision.HIGHEST,
        preferred_element_type=jnp.float32,
    )
    state = (cmax_part, csum_part, beam_part, lmax_part, lsum_part, accum_part)
    row_count = query_count // groups
    merged = merged_2(state, "cluster", combine_states)
    row_start = lax.axis_index("cluster") * row_count
    own = tuple((lax.dynamic_slice_in_dim(member, row_start, row_count, 0) for member in merged))
    cmax_own, csum_own, beam_own, lmax_own, lsum_own, accum_own = own
    lse = cmax_own + jnp.log(csum_own)
    beam_logprob = beam_own - lse[:, None]
    readout = (accum_own / lsum_own[:, None]).astype(jnp.bfloat16)
    return (readout, beam_logprob)


MESH = pl.DeviceIdType.MESH
CODE_MAX = 32767.0
LANES = 128


def fused_kernel(
    groups,
    capacity,
    q_ref,
    cent_ref,
    leaves_ref,
    beam_ref,
    readout_ref,
    logprob_ref,
    block,
    cent_buf,
    beam_buf,
    leaf_buf,
    centroid_send,
    centroid_recv,
    stat_send,
    stat_recv,
    code_send,
    code_recv,
    leaf_sem,
    own_sem,
    q_send_sem,
    q_recv_sem,
    centroid_send_sem,
    centroid_recv_sem,
    stat_send_sem,
    stat_recv_sem,
    code_send_sem,
    code_recv_sem,
):
    rows, width = q_ref.shape
    clusters = cent_ref.shape[0]
    total = groups * rows
    beam_width = beam_ref.shape[0]
    chips = groups // 2
    score_scale = 1.0 / math.sqrt(width)
    f32 = jnp.float32
    me = lax.axis_index("cluster")
    chip, core = me // 2, me % 2
    sibling = chip * 2 + (1 - core)
    first = me * clusters

    def peer_at(offset, side):
        return lax.rem(chip + offset, chips) * 2 + side

    peers = [peer_at(o, s) for o in range(1, chips) for s in (core, 1 - core)] + [sibling]

    def signal_peers():
        barrier = pltpu.get_barrier_semaphore()
        for peer in peers:
            pl.semaphore_signal(barrier, inc=1, device_id={"cluster": peer}, device_id_type=MESH)
        pl.semaphore_wait(barrier, len(peers))

    own_copies = [
        pltpu.make_async_copy(q_ref, block.at[me], own_sem.at[0]),
        pltpu.make_async_copy(beam_ref, beam_buf, own_sem.at[1]),
        pltpu.make_async_copy(cent_ref, cent_buf, own_sem.at[2]),
    ]
    leaf_copies = [
        pltpu.make_async_copy(leaves_ref.at[c], leaf_buf.at[c], leaf_sem.at[c])
        for c in range(clusters)
    ]
    for copy in own_copies + leaf_copies:
        copy.start()
    signal_peers()

    def push(src, dst, send_sem, recv_sem, peer):
        return pltpu.make_async_remote_copy(
            src_ref=src,
            dst_ref=dst,
            send_sem=send_sem,
            recv_sem=recv_sem,
            device_id={"cluster": peer},
            device_id_type=MESH,
        )

    own_copies[0].wait()
    mine = block.at[me]
    sends = []
    for number, offset in enumerate(range(1, chips)):
        peer = peer_at(offset, core)
        sends.append(push(mine, mine, q_send_sem.at[number], q_recv_sem.at[me], peer))
    sends.append(push(mine, mine, q_send_sem.at[chips - 1], q_recv_sem.at[me], sibling))
    for copy in sends:
        copy.start()

    own_copies[1].wait()
    beams = beam_buf[...]
    members = jnp.concatenate(
        [
            jnp.max((beams == first + c).astype(f32), axis=0, keepdims=True)
            for c in range(clusters)
        ],
        axis=0,
    )
    upper = (
        lax.broadcasted_iota(jnp.int32, (total, total), 0)
        <= lax.broadcasted_iota(jnp.int32, (total, total), 1)
    ).astype(jnp.bfloat16)
    padded = jnp.concatenate([members, jnp.zeros((LANES - clusters, total), f32)], axis=0)
    counts = jnp.dot(padded.astype(jnp.bfloat16), upper, preferred_element_type=f32)
    slots = jnp.where(padded > 0.0, counts, 0.0)
    slot_number = lax.broadcasted_iota(jnp.int32, (capacity, total), 0).astype(f32) + 1.0
    dispatch = jnp.concatenate(
        [(slots[c : c + 1, :] == slot_number).astype(f32) for c in range(clusters)], axis=0
    )
    slot_total = clusters * capacity
    slots_down = slots.T
    slot_across = lax.broadcasted_iota(jnp.int32, (total, slot_total), 1)
    wanted = jnp.concatenate(
        [jnp.broadcast_to(slots_down[:, c : c + 1], (total, capacity)) for c in range(clusters)],
        axis=1,
    )
    collect = (wanted == (slot_across % capacity).astype(f32) + 1.0).astype(jnp.bfloat16)

    def arrival(origin):
        return push(block.at[origin], block.at[origin], q_send_sem.at[0], q_recv_sem.at[origin], sibling)

    for offset in range(1, chips):
        origin = peer_at(chips - offset, core)
        arrival(origin).wait_recv()
        relay = push(
            block.at[origin],
            block.at[origin],
            q_send_sem.at[chips - 1 + offset],
            q_recv_sem.at[origin],
            sibling,
        )
        relay.start()
        sends.append(relay)
    arrival(sibling).wait_recv()
    for offset in range(1, chips):
        arrival(peer_at(chips - offset, 1 - core)).wait_recv()
    own_copies[2].wait()

    queries = block[...].reshape(total, width)
    cent = jnp.concatenate(
        [cent_buf[...], jnp.zeros((LANES - clusters, width), cent_buf.dtype)], axis=0
    )
    nt = (((1,), (1,)), ((), ()))
    cscore = lax.dot_general(cent, queries, nt, preferred_element_type=f32)[0:clusters]
    cscore = cscore * score_scale
    part_max = jnp.max(cscore, axis=0, keepdims=True)
    part_sum = jnp.sum(jnp.exp(cscore - part_max), axis=0, keepdims=True)
    picks = sum(
        jnp.where(beams == first + c, cscore[c : c + 1, :], 0.0) for c in range(clusters)
    )
    for g in range(groups):
        lanes = slice(g * rows, (g + 1) * rows)
        centroid_send[g, 0:beam_width, 0:rows] = picks[:, lanes]
        centroid_send[g, beam_width : beam_width + 1, 0:rows] = part_max[:, lanes]
        centroid_send[g, beam_width + 1 : beam_width + 2, 0:rows] = part_sum[:, lanes]
    centroid_copies = [
        push(
            centroid_send.at[peer],
            centroid_recv.at[me],
            centroid_send_sem.at[number],
            centroid_recv_sem.at[me],
            peer,
        )
        for number, peer in enumerate(peers)
    ]
    for copy in centroid_copies:
        copy.start()

    picked = jnp.dot(
        dispatch.astype(jnp.bfloat16), queries, preferred_element_type=f32
    ).astype(jnp.bfloat16)
    lane = lax.broadcasted_iota(jnp.int32, (slot_total, LANES), 1)
    owner = lax.broadcasted_iota(jnp.int32, (slot_total, LANES), 0) // capacity
    slot_scores = lax.dot_general(picked, cent, nt, preferred_element_type=f32) * score_scale
    slot_centroid = jnp.sum(jnp.where(lane == owner, slot_scores, 0.0), axis=1, keepdims=True)
    for copy in leaf_copies:
        copy.wait()

    def scores(c):
        return lax.dot_general(
            picked[c * capacity : (c + 1) * capacity],
            leaf_buf[c],
            nt,
            preferred_element_type=f32,
        )

    peaks, masses, sums = [], [], []
    current = scores(0)
    for c in range(clusters):
        upcoming = scores(c + 1) if c + 1 < clusters else None
        peak = jnp.max(current, axis=1, keepdims=True)
        weights = jnp.exp((current - peak) * score_scale)
        masses.append(jnp.sum(weights, axis=1, keepdims=True))
        peaks.append(peak)
        sums.append(
            jnp.dot(weights.astype(jnp.bfloat16), leaf_buf[c], preferred_element_type=f32)
        )
        current = upcoming
    level = jnp.concatenate(peaks, axis=0) * score_scale + slot_centroid
    mass = jnp.concatenate(masses, axis=0)
    summed = jnp.concatenate(sums, axis=0)

    used = dispatch > 0.0
    top = jnp.max(jnp.where(used, level, floor_value), axis=0, keepdims=True)
    slot_top = jnp.max(jnp.where(used, top, floor_value), axis=1, keepdims=True)
    filled = jnp.max(dispatch, axis=1, keepdims=True) > 0.0
    gain = jnp.where(filled, jnp.exp(jnp.where(filled, level - slot_top, 0.0)), 0.0)
    denom = jnp.sum(jnp.where(used, mass * gain, 0.0), axis=0, keepdims=True)
    scaled = summed * gain
    coarse = scaled.astype(jnp.bfloat16)
    fine = (scaled - coarse.astype(f32)).astype(jnp.bfloat16)
    held = jnp.dot(collect, coarse, preferred_element_type=f32) + jnp.dot(
        collect, fine, preferred_element_type=f32
    )
    largest = jnp.maximum(jnp.max(jnp.abs(held), axis=1, keepdims=True), 1e-30)
    coded = jnp.round(held * (CODE_MAX / largest)).astype(jnp.int32).astype(jnp.int16)
    code_send[...] = coded.reshape(groups, rows, width)
    steps = jnp.broadcast_to(largest * (1.0 / CODE_MAX), (total, LANES)).T
    for g in range(groups):
        lanes = slice(g * rows, (g + 1) * rows)
        stat_send[g, 0:1, 0:rows] = top[:, lanes]
        stat_send[g, 1:2, 0:rows] = denom[:, lanes]
        stat_send[g, 2:3, 0:rows] = steps[0:1, lanes]

    result_copies = []
    for number, peer in enumerate(peers):
        result_copies.append(
            push(
                stat_send.at[peer],
                stat_recv.at[me],
                stat_send_sem.at[number],
                stat_recv_sem.at[me],
                peer,
            )
        )
        result_copies.append(
            push(
                code_send.at[peer],
                code_recv.at[me],
                code_send_sem.at[number],
                code_recv_sem.at[me],
                peer,
            )
        )
    for copy in result_copies:
        copy.start()

    for number, peer in enumerate(peers):
        push(
            centroid_send.at[peer],
            centroid_recv.at[peer],
            centroid_send_sem.at[number],
            centroid_recv_sem.at[peer],
            peer,
        ).wait_recv()
    centroid_recv[me] = centroid_send[me]
    parts = [centroid_recv[g] for g in range(groups)]
    cmax = functools.reduce(jnp.maximum, [p[beam_width : beam_width + 1] for p in parts])
    csum = sum(
        p[beam_width + 1 : beam_width + 2] * jnp.exp(p[beam_width : beam_width + 1] - cmax)
        for p in parts
    )
    logprob = sum(p[0:beam_width] for p in parts) - (cmax + jnp.log(csum))
    logprob_ref[...] = logprob[:, 0:rows]

    for number, peer in enumerate(peers):
        push(
            stat_send.at[peer],
            stat_recv.at[peer],
            stat_send_sem.at[number],
            stat_recv_sem.at[peer],
            peer,
        ).wait_recv()
    stat_recv[me] = stat_send[me]
    code_recv[me] = code_send[me]
    tops = stat_recv[:, 0, :]
    overall = jnp.max(tops, axis=0, keepdims=True)
    factors = jnp.exp(tops - overall)
    whole = jnp.sum(factors * stat_recv[:, 1, :], axis=0, keepdims=True)
    shares = factors * stat_recv[:, 2, :] / whole
    shares = jnp.concatenate([shares, jnp.zeros((LANES - groups, LANES), f32)], axis=0).T[0:rows]

    for number, peer in enumerate(peers):
        push(
            code_send.at[peer],
            code_recv.at[peer],
            code_send_sem.at[number],
            code_recv_sem.at[peer],
            peer,
        ).wait_recv()
    merged = jnp.zeros((rows, width), f32)
    for g in range(groups):
        merged = merged + code_recv[g].astype(jnp.int32).astype(f32) * shares[:, g : g + 1]
    readout_ref[...] = merged.astype(jnp.bfloat16)

    for copy in sends + centroid_copies + result_copies:
        copy.wait_send()


def fused(queries, centroids, leaves, beam):
    groups = lax.axis_size("cluster")
    rows, width = queries.shape
    clusters = centroids.shape[0]
    total, beam_width = beam.shape
    capacity = 2 * total * beam_width // (clusters * groups)
    if rows % 16 or capacity % 16 or groups % 2 or groups > 16 or rows > LANES or beam_width != 8:
        return per_device(queries, centroids, leaves, beam)
    vmem = pl.BlockSpec(memory_space=pltpu.VMEM)
    hbm = pl.BlockSpec(memory_space=pltpu.HBM)
    dma = pltpu.SemaphoreType.DMA
    peers = groups - 1
    readout, logprob = pl.pallas_call(
        functools.partial(fused_kernel, groups, capacity),
        out_shape=(
            jax.ShapeDtypeStruct((rows, width), jnp.bfloat16),
            jax.ShapeDtypeStruct((beam_width, rows), jnp.float32),
        ),
        in_specs=[hbm, hbm, hbm, hbm],
        out_specs=(vmem, vmem),
        scratch_shapes=[
            pltpu.VMEM((groups, rows, width), jnp.bfloat16),
            pltpu.VMEM(centroids.shape, jnp.bfloat16),
            pltpu.VMEM((beam_width, total), jnp.int32),
            pltpu.VMEM(leaves.shape, jnp.bfloat16),
            pltpu.VMEM((groups, beam_width + 8, LANES), jnp.float32),
            pltpu.VMEM((groups, beam_width + 8, LANES), jnp.float32),
            pltpu.VMEM((groups, 8, LANES), jnp.float32),
            pltpu.VMEM((groups, 8, LANES), jnp.float32),
            pltpu.VMEM((groups, rows, width), jnp.int16),
            pltpu.VMEM((groups, rows, width), jnp.int16),
            dma((clusters,)),
            dma((3,)),
            dma((groups,)),
            dma((groups,)),
            dma((peers,)),
            dma((groups,)),
            dma((peers,)),
            dma((groups,)),
            dma((peers,)),
            dma((groups,)),
        ],
        compiler_params=pltpu.CompilerParams(
            collective_id=0, has_side_effects=True, vmem_limit_bytes=64 * 1024 * 1024
        ),
    )(queries, centroids, leaves, beam.T)
    return readout, logprob.T


def solution(mesh):
    return jax.shard_map(
        fused,
        mesh=mesh,
        in_specs=(
            P(("query", "cluster"), None),
            P("cluster", None),
            P("cluster", None, None),
            P("query", None),
        ),
        out_specs=(P(("query", "cluster"), None), P(("query", "cluster"), None)),
        check_vma=False,
    )
```

```python
import functools
import math

import jax
import jax.numpy as jnp
from jax import lax
from jax.experimental import pallas as pl
from jax.experimental.pallas import tpu as pltpu
from jax.sharding import PartitionSpec as P

floor_value = -1e30


def merged_2(part, axis, combine):
    gathered = jax.tree.map(lambda a: lax.all_gather(a, axis), part)

    def take(source):
        return jax.tree.map(lambda a: lax.dynamic_index_in_dim(a, source, 0, False), gathered)

    return lax.fori_loop(
        1, lax.axis_size(axis), lambda source, state: combine(state, take(source)), take(0)
    )


def combine_states(first, second):
    cmax_one, csum_one, beam_one, lmax_one, lsum_one, accum_one = first
    cmax_two, csum_two, beam_two, lmax_two, lsum_two, accum_two = second
    cmax_new = jnp.maximum(cmax_one, cmax_two)
    csum_new = csum_one * jnp.exp(cmax_one - cmax_new) + csum_two * jnp.exp(cmax_two - cmax_new)
    lmax_new = jnp.maximum(lmax_one, lmax_two)
    factor_one = jnp.exp(lmax_one - lmax_new)
    factor_two = jnp.exp(lmax_two - lmax_new)
    lsum_new = lsum_one * factor_one + lsum_two * factor_two
    accum_new = accum_one * factor_one[:, None] + accum_two * factor_two[:, None]
    return (cmax_new, csum_new, beam_one + beam_two, lmax_new, lsum_new, accum_new)


def per_device(queries, centroids, leaves, beam):
    groups = lax.axis_size("cluster")
    query_block = lax.all_gather(queries, "cluster", axis=0, tiled=True)
    query_count, model_width = query_block.shape
    cluster_count, leaf_count, unused_width = leaves.shape
    beam_width = beam.shape[1]
    score_scale = 1.0 / math.sqrt(model_width)
    first_cluster = lax.axis_index("cluster") * cluster_count
    cscore = jnp.dot(query_block, centroids.T, preferred_element_type=jnp.float32) * score_scale
    cmax_part = jnp.max(cscore, axis=1)
    csum_part = jnp.sum(jnp.exp(cscore - cmax_part[:, None]), axis=1)
    owned = first_cluster + jnp.arange(cluster_count, dtype=jnp.int32)
    matches = beam[:, :, None] == owned[None, None, :]
    beam_part = jnp.sum(jnp.where(matches, cscore[:, None, :], 0.0), axis=2)
    membership = jnp.any(matches, axis=1).astype(jnp.int32)
    slot_index = jnp.cumsum(membership, axis=0) - 1
    capacity = max(4, 2 * query_count * beam_width // (cluster_count * groups))
    positions = jnp.arange(capacity, dtype=jnp.int32)
    dispatch = (membership.T[:, None, :] == 1) & (
        slot_index.T[:, None, :] == positions[None, :, None]
    )
    picked = jnp.einsum(
        "csq,qd->csd",
        dispatch.astype(jnp.bfloat16),
        query_block,
        preferred_element_type=jnp.float32,
    ).astype(jnp.bfloat16)
    slot_centroid = jnp.sum(jnp.where(dispatch, cscore.T[:, None, :], 0.0), axis=2)
    logits = (
        jnp.einsum("csd,cjd->csj", picked, leaves, preferred_element_type=jnp.float32) * score_scale
    )
    logits = logits + slot_centroid[:, :, None]
    slot_max = jnp.max(logits, axis=2)
    weights = jnp.exp(logits - slot_max[:, :, None])
    slot_sum = jnp.sum(weights, axis=2)
    slot_accum = jnp.einsum(
        "csj,cjd->csd", weights.astype(jnp.bfloat16), leaves, preferred_element_type=jnp.float32
    )
    slot_total = cluster_count * capacity
    dispatch_flat = dispatch.reshape(slot_total, query_count)
    slot_max_flat = slot_max.reshape(slot_total)
    masked_max = jnp.where(dispatch_flat, slot_max_flat[:, None], floor_value)
    lmax_part = jnp.max(masked_max, axis=0)
    exponent = jnp.where(dispatch_flat, slot_max_flat[:, None] - lmax_part[None, :], 0.0)
    factors = jnp.where(dispatch_flat, jnp.exp(exponent), 0.0)
    lsum_part = jnp.sum(factors * slot_sum.reshape(slot_total)[:, None], axis=0)
    accum_part = jnp.dot(
        factors.T,
        slot_accum.reshape(slot_total, model_width),
        precision=lax.Precision.HIGHEST,
        preferred_element_type=jnp.float32,
    )
    state = (cmax_part, csum_part, beam_part, lmax_part, lsum_part, accum_part)
    row_count = query_count // groups
    merged = merged_2(state, "cluster", combine_states)
    row_start = lax.axis_index("cluster") * row_count
    own = tuple((lax.dynamic_slice_in_dim(member, row_start, row_count, 0) for member in merged))
    cmax_own, csum_own, beam_own, lmax_own, lsum_own, accum_own = own
    lse = cmax_own + jnp.log(csum_own)
    beam_logprob = beam_own - lse[:, None]
    readout = (accum_own / lsum_own[:, None]).astype(jnp.bfloat16)
    return (readout, beam_logprob)


MESH = pl.DeviceIdType.MESH
CODE_MAX = 32767.0
LANES = 128


def fused_kernel(
    groups,
    capacity,
    q_ref,
    cent_ref,
    leaves_ref,
    beam_ref,
    readout_ref,
    logprob_ref,
    block,
    cent_buf,
    beam_buf,
    leaf_buf,
    centroid_send,
    centroid_recv,
    held_buf,
    near_recv,
    level_buf,
    near_level,
    stat_send,
    stat_recv,
    code_send,
    code_recv,
    leaf_sem,
    own_sem,
    q_send_sem,
    q_recv_sem,
    centroid_send_sem,
    centroid_recv_sem,
    near_send_sem,
    near_recv_sem,
    stat_send_sem,
    stat_recv_sem,
    code_send_sem,
    code_recv_sem,
):
    rows, width = q_ref.shape
    clusters = cent_ref.shape[0]
    total = groups * rows
    beam_width = beam_ref.shape[0]
    chips = groups // 2
    score_scale = 1.0 / math.sqrt(width)
    f32 = jnp.float32
    me = lax.axis_index("cluster")
    chip, core = me // 2, me % 2
    sibling = chip * 2 + (1 - core)
    first = me * clusters

    def peer_at(offset, side):
        return lax.rem(chip + offset, chips) * 2 + side

    peers = [peer_at(o, s) for o in range(1, chips) for s in (core, 1 - core)] + [sibling]

    def signal_peers():
        barrier = pltpu.get_barrier_semaphore()
        for peer in peers:
            pl.semaphore_signal(barrier, inc=1, device_id={"cluster": peer}, device_id_type=MESH)
        pl.semaphore_wait(barrier, len(peers))

    own_copies = [
        pltpu.make_async_copy(q_ref, block.at[me], own_sem.at[0]),
        pltpu.make_async_copy(beam_ref, beam_buf, own_sem.at[1]),
        pltpu.make_async_copy(cent_ref, cent_buf, own_sem.at[2]),
    ]
    leaf_copies = [
        pltpu.make_async_copy(leaves_ref.at[c], leaf_buf.at[c], leaf_sem.at[c])
        for c in range(clusters)
    ]
    for copy in own_copies + leaf_copies:
        copy.start()
    signal_peers()

    def push(src, dst, send_sem, recv_sem, peer):
        return pltpu.make_async_remote_copy(
            src_ref=src,
            dst_ref=dst,
            send_sem=send_sem,
            recv_sem=recv_sem,
            device_id={"cluster": peer},
            device_id_type=MESH,
        )

    own_copies[0].wait()
    mine = block.at[me]
    sends = []
    for number, offset in enumerate(range(1, chips)):
        peer = peer_at(offset, core)
        sends.append(push(mine, mine, q_send_sem.at[number], q_recv_sem.at[me], peer))
    sends.append(push(mine, mine, q_send_sem.at[chips - 1], q_recv_sem.at[me], sibling))
    for copy in sends:
        copy.start()

    own_copies[1].wait()
    beams = beam_buf[...]
    members = jnp.concatenate(
        [
            jnp.max((beams == first + c).astype(f32), axis=0, keepdims=True)
            for c in range(clusters)
        ],
        axis=0,
    )
    upper = (
        lax.broadcasted_iota(jnp.int32, (total, total), 0)
        <= lax.broadcasted_iota(jnp.int32, (total, total), 1)
    ).astype(jnp.bfloat16)
    padded = jnp.concatenate([members, jnp.zeros((LANES - clusters, total), f32)], axis=0)
    counts = jnp.dot(padded.astype(jnp.bfloat16), upper, preferred_element_type=f32)
    slots = jnp.where(padded > 0.0, counts, 0.0)
    slot_number = lax.broadcasted_iota(jnp.int32, (capacity, total), 0).astype(f32) + 1.0
    dispatch = jnp.concatenate(
        [(slots[c : c + 1, :] == slot_number).astype(f32) for c in range(clusters)], axis=0
    )
    slot_total = clusters * capacity
    slots_down = slots.T
    slot_across = lax.broadcasted_iota(jnp.int32, (total, slot_total), 1)
    wanted = jnp.concatenate(
        [jnp.broadcast_to(slots_down[:, c : c + 1], (total, capacity)) for c in range(clusters)],
        axis=1,
    )
    collect = (wanted == (slot_across % capacity).astype(f32) + 1.0).astype(jnp.bfloat16)

    def arrival(origin):
        return push(block.at[origin], block.at[origin], q_send_sem.at[0], q_recv_sem.at[origin], sibling)

    for offset in range(1, chips):
        origin = peer_at(chips - offset, core)
        arrival(origin).wait_recv()
        relay = push(
            block.at[origin],
            block.at[origin],
            q_send_sem.at[chips - 1 + offset],
            q_recv_sem.at[origin],
            sibling,
        )
        relay.start()
        sends.append(relay)
    arrival(sibling).wait_recv()
    for offset in range(1, chips):
        arrival(peer_at(chips - offset, 1 - core)).wait_recv()
    own_copies[2].wait()

    queries = block[...].reshape(total, width)
    cent = jnp.concatenate(
        [cent_buf[...], jnp.zeros((LANES - clusters, width), cent_buf.dtype)], axis=0
    )
    nt = (((1,), (1,)), ((), ()))
    cscore = lax.dot_general(cent, queries, nt, preferred_element_type=f32)[0:clusters]
    cscore = cscore * score_scale
    part_max = jnp.max(cscore, axis=0, keepdims=True)
    part_sum = jnp.sum(jnp.exp(cscore - part_max), axis=0, keepdims=True)
    picks = sum(
        jnp.where(beams == first + c, cscore[c : c + 1, :], 0.0) for c in range(clusters)
    )
    for g in range(groups):
        lanes = slice(g * rows, (g + 1) * rows)
        centroid_send[g, 0:beam_width, 0:rows] = picks[:, lanes]
        centroid_send[g, beam_width : beam_width + 1, 0:rows] = part_max[:, lanes]
        centroid_send[g, beam_width + 1 : beam_width + 2, 0:rows] = part_sum[:, lanes]
    centroid_copies = [
        push(
            centroid_send.at[peer],
            centroid_recv.at[me],
            centroid_send_sem.at[number],
            centroid_recv_sem.at[me],
            peer,
        )
        for number, peer in enumerate(peers)
    ]
    for copy in centroid_copies:
        copy.start()

    picked = jnp.dot(
        dispatch.astype(jnp.bfloat16), queries, preferred_element_type=f32
    ).astype(jnp.bfloat16)
    lane = lax.broadcasted_iota(jnp.int32, (slot_total, LANES), 1)
    owner = lax.broadcasted_iota(jnp.int32, (slot_total, LANES), 0) // capacity
    slot_scores = lax.dot_general(picked, cent, nt, preferred_element_type=f32) * score_scale
    slot_centroid = jnp.sum(jnp.where(lane == owner, slot_scores, 0.0), axis=1, keepdims=True)
    for copy in leaf_copies:
        copy.wait()

    def scores(c):
        return lax.dot_general(
            picked[c * capacity : (c + 1) * capacity],
            leaf_buf[c],
            nt,
            preferred_element_type=f32,
        )

    peaks, masses, sums = [], [], []
    current = scores(0)
    for c in range(clusters):
        upcoming = scores(c + 1) if c + 1 < clusters else None
        peak = jnp.max(current, axis=1, keepdims=True)
        weights = jnp.exp((current - peak) * score_scale)
        masses.append(jnp.sum(weights, axis=1, keepdims=True))
        peaks.append(peak)
        sums.append(
            jnp.dot(weights.astype(jnp.bfloat16), leaf_buf[c], preferred_element_type=f32)
        )
        current = upcoming
    level = jnp.concatenate(peaks, axis=0) * score_scale + slot_centroid
    mass = jnp.concatenate(masses, axis=0)
    summed = jnp.concatenate(sums, axis=0)

    used = dispatch > 0.0
    top = jnp.max(jnp.where(used, level, floor_value), axis=0, keepdims=True)
    slot_top = jnp.max(jnp.where(used, top, floor_value), axis=1, keepdims=True)
    filled = jnp.max(dispatch, axis=1, keepdims=True) > 0.0
    gain = jnp.where(filled, jnp.exp(jnp.where(filled, level - slot_top, 0.0)), 0.0)
    denom = jnp.sum(jnp.where(used, mass * gain, 0.0), axis=0, keepdims=True)
    scaled = summed * gain
    coarse = scaled.astype(jnp.bfloat16)
    fine = (scaled - coarse.astype(f32)).astype(jnp.bfloat16)
    held = jnp.dot(collect, coarse, preferred_element_type=f32) + jnp.dot(
        collect, fine, preferred_element_type=f32
    )
    for g in range(groups):
        lanes = slice(g * rows, (g + 1) * rows)
        level_buf[g % 2, g // 2, 0:1, 0:rows] = top[:, lanes]
        level_buf[g % 2, g // 2, 1:2, 0:rows] = denom[:, lanes]
        held_buf[g % 2, g // 2] = held[lanes]
    order = [2, 1, 3, 0] if chips == 4 else list(range(1, chips)) + [0]
    near_copies = [
        push(
            level_buf.at[1 - core],
            near_level,
            near_send_sem.at[chips],
            near_recv_sem.at[chips],
            sibling,
        )
    ]
    for offset in order:
        g = lax.rem(chip + offset, chips)
        near_copies.append(
            push(
                held_buf.at[1 - core, g],
                near_recv.at[g],
                near_send_sem.at[offset],
                near_recv_sem.at[g],
                sibling,
            )
        )
    for copy in near_copies:
        copy.start()

    near_copies[0].wait_recv()
    diagonal = lax.broadcasted_iota(jnp.int32, (rows, LANES), 0) == lax.broadcasted_iota(
        jnp.int32, (rows, LANES), 1
    )

    def to_column(row):
        return jnp.sum(jnp.where(diagonal, row, 0.0), axis=1, keepdims=True)

    def to_row(column):
        return jnp.sum(jnp.where(diagonal, column, 0.0), axis=0, keepdims=True)

    result_copies = []
    for number, offset in enumerate(order):
        g = lax.rem(chip + offset, chips)
        here, near = level_buf[core, g], near_level[g]
        high = jnp.maximum(here[0:1], near[0:1])
        here_gain, near_gain = jnp.exp(here[0:1] - high), jnp.exp(near[0:1] - high)
        amount = here[1:2] * here_gain + near[1:2] * near_gain
        push(
            held_buf.at[1 - core, g],
            near_recv.at[g],
            near_send_sem.at[offset],
            near_recv_sem.at[g],
            sibling,
        ).wait_recv()
        both = held_buf[core, g] * to_column(here_gain) + near_recv[g] * to_column(near_gain)
        if offset == 0:
            own_high, own_amount, own_both = high, amount, both
            continue
        largest = jnp.maximum(jnp.max(jnp.abs(both), axis=1, keepdims=True), 1e-30)
        code_send[number] = (
            jnp.round(both * (CODE_MAX / largest)).astype(jnp.int32).astype(jnp.int16)
        )
        stat_send[number, 0:1] = high
        stat_send[number, 1:2] = amount
        stat_send[number, 2:3] = to_row(largest * (1.0 / CODE_MAX))
        peer = g * 2 + core
        for buffers, sems in (
            ((stat_send, stat_recv), (stat_send_sem, stat_recv_sem)),
            ((code_send, code_recv), (code_send_sem, code_recv_sem)),
        ):
            copy = push(
                buffers[0].at[number], buffers[1].at[chip], sems[0].at[number], sems[1].at[chip], peer
            )
            copy.start()
            result_copies.append(copy)

    for number, peer in enumerate(peers):
        push(
            centroid_send.at[peer],
            centroid_recv.at[peer],
            centroid_send_sem.at[number],
            centroid_recv_sem.at[peer],
            peer,
        ).wait_recv()
    centroid_recv[me] = centroid_send[me]
    parts = [centroid_recv[g] for g in range(groups)]
    cmax = functools.reduce(jnp.maximum, [p[beam_width : beam_width + 1] for p in parts])
    csum = sum(
        p[beam_width + 1 : beam_width + 2] * jnp.exp(p[beam_width : beam_width + 1] - cmax)
        for p in parts
    )
    logprob = sum(p[0:beam_width] for p in parts) - (cmax + jnp.log(csum))
    logprob_ref[...] = logprob[:, 0:rows]

    sources = [lax.rem(chip + offset, chips) for offset in range(1, chips)]
    for g in sources:
        push(stat_send.at[0], stat_recv.at[g], stat_send_sem.at[0], stat_recv_sem.at[g], sibling).wait_recv()
    stats = [stat_recv[g] for g in sources]
    overall = functools.reduce(jnp.maximum, [t[0:1] for t in stats], own_high)
    own_share = jnp.exp(own_high - overall)
    shares = [jnp.exp(t[0:1] - overall) for t in stats]
    whole = own_amount * own_share + sum(f * t[1:2] for f, t in zip(shares, stats))
    merged = own_both * to_column(own_share / whole)
    for g, share, stat in zip(sources, shares, stats):
        push(code_send.at[0], code_recv.at[g], code_send_sem.at[0], code_recv_sem.at[g], sibling).wait_recv()
        merged = merged + code_recv[g].astype(jnp.int32).astype(f32) * to_column(
            share * stat[2:3] / whole
        )
    readout_ref[...] = merged.astype(jnp.bfloat16)

    for copy in sends + centroid_copies + near_copies + result_copies:
        copy.wait_send()


def store_kernel(readout_ref, logprob_ref, readout_out, logprob_out, sems):
    copies = [
        pltpu.make_async_copy(readout_ref, readout_out, sems.at[0]),
        pltpu.make_async_copy(logprob_ref, logprob_out, sems.at[1]),
    ]
    for copy in copies:
        copy.start()
    for copy in copies:
        copy.wait()


def fused(queries, centroids, leaves, beam):
    groups = lax.axis_size("cluster")
    rows, width = queries.shape
    clusters = centroids.shape[0]
    total, beam_width = beam.shape
    capacity = 2 * total * beam_width // (clusters * groups)
    if rows % 16 or capacity % 16 or groups % 2 or groups > 16 or rows > LANES or beam_width != 8:
        return per_device(queries, centroids, leaves, beam)
    vmem = pl.BlockSpec(memory_space=pltpu.VMEM)
    hbm = pl.BlockSpec(memory_space=pltpu.HBM)
    dma = pltpu.SemaphoreType.DMA
    peers = groups - 1
    chips = groups // 2
    readout, logprob = pl.pallas_call(
        functools.partial(fused_kernel, groups, capacity),
        out_shape=(
            jax.ShapeDtypeStruct((rows, width), jnp.bfloat16),
            jax.ShapeDtypeStruct((beam_width, rows), jnp.float32),
        ),
        in_specs=[hbm, hbm, hbm, hbm],
        out_specs=(vmem, vmem),
        scratch_shapes=[
            pltpu.VMEM((groups, rows, width), jnp.bfloat16),
            pltpu.VMEM(centroids.shape, jnp.bfloat16),
            pltpu.VMEM((beam_width, total), jnp.int32),
            pltpu.VMEM(leaves.shape, jnp.bfloat16),
            pltpu.VMEM((groups, beam_width + 8, LANES), jnp.float32),
            pltpu.VMEM((groups, beam_width + 8, LANES), jnp.float32),
            pltpu.VMEM((2, chips, rows, width), jnp.float32),
            pltpu.VMEM((chips, rows, width), jnp.float32),
            pltpu.VMEM((2, chips, 8, LANES), jnp.float32),
            pltpu.VMEM((chips, 8, LANES), jnp.float32),
            pltpu.VMEM((chips, 8, LANES), jnp.float32),
            pltpu.VMEM((chips, 8, LANES), jnp.float32),
            pltpu.VMEM((chips, rows, width), jnp.int16),
            pltpu.VMEM((chips, rows, width), jnp.int16),
            dma((clusters,)),
            dma((3,)),
            dma((groups,)),
            dma((groups,)),
            dma((peers,)),
            dma((groups,)),
            dma((chips + 1,)),
            dma((chips + 1,)),
            dma((chips,)),
            dma((chips,)),
            dma((chips,)),
            dma((chips,)),
        ],
        compiler_params=pltpu.CompilerParams(
            collective_id=0, has_side_effects=True, vmem_limit_bytes=64 * 1024 * 1024
        ),
    )(queries, centroids, leaves, beam.T)
    readout, logprob = pl.pallas_call(
        store_kernel,
        out_shape=(
            jax.ShapeDtypeStruct(readout.shape, readout.dtype),
            jax.ShapeDtypeStruct(logprob.shape, logprob.dtype),
        ),
        in_specs=[hbm, hbm],
        out_specs=(hbm, hbm),
        scratch_shapes=[dma((2,))],
        compiler_params=pltpu.CompilerParams(vmem_limit_bytes=64 * 1024 * 1024),
    )(readout, logprob)
    return readout, logprob.T


def solution(mesh):
    return jax.shard_map(
        fused,
        mesh=mesh,
        in_specs=(
            P(("query", "cluster"), None),
            P("cluster", None),
            P("cluster", None, None),
            P("query", None),
        ),
        out_specs=(P(("query", "cluster"), None), P(("query", "cluster"), None)),
        check_vma=False,
    )
```

```python
import functools
import math

import jax
import jax.numpy as jnp
from jax import lax
from jax.experimental import pallas as pl
from jax.experimental.pallas import tpu as pltpu
from jax.sharding import PartitionSpec as P

floor_value = -1e30


def merged_2(part, axis, combine):
    gathered = jax.tree.map(lambda a: lax.all_gather(a, axis), part)

    def take(source):
        return jax.tree.map(lambda a: lax.dynamic_index_in_dim(a, source, 0, False), gathered)

    return lax.fori_loop(
        1, lax.axis_size(axis), lambda source, state: combine(state, take(source)), take(0)
    )


def combine_states(first, second):
    cmax_one, csum_one, beam_one, lmax_one, lsum_one, accum_one = first
    cmax_two, csum_two, beam_two, lmax_two, lsum_two, accum_two = second
    cmax_new = jnp.maximum(cmax_one, cmax_two)
    csum_new = csum_one * jnp.exp(cmax_one - cmax_new) + csum_two * jnp.exp(cmax_two - cmax_new)
    lmax_new = jnp.maximum(lmax_one, lmax_two)
    factor_one = jnp.exp(lmax_one - lmax_new)
    factor_two = jnp.exp(lmax_two - lmax_new)
    lsum_new = lsum_one * factor_one + lsum_two * factor_two
    accum_new = accum_one * factor_one[:, None] + accum_two * factor_two[:, None]
    return (cmax_new, csum_new, beam_one + beam_two, lmax_new, lsum_new, accum_new)


def per_device(queries, centroids, leaves, beam):
    groups = lax.axis_size("cluster")
    query_block = lax.all_gather(queries, "cluster", axis=0, tiled=True)
    query_count, model_width = query_block.shape
    cluster_count, leaf_count, unused_width = leaves.shape
    beam_width = beam.shape[1]
    score_scale = 1.0 / math.sqrt(model_width)
    first_cluster = lax.axis_index("cluster") * cluster_count
    cscore = jnp.dot(query_block, centroids.T, preferred_element_type=jnp.float32) * score_scale
    cmax_part = jnp.max(cscore, axis=1)
    csum_part = jnp.sum(jnp.exp(cscore - cmax_part[:, None]), axis=1)
    owned = first_cluster + jnp.arange(cluster_count, dtype=jnp.int32)
    matches = beam[:, :, None] == owned[None, None, :]
    beam_part = jnp.sum(jnp.where(matches, cscore[:, None, :], 0.0), axis=2)
    membership = jnp.any(matches, axis=1).astype(jnp.int32)
    slot_index = jnp.cumsum(membership, axis=0) - 1
    capacity = max(4, 2 * query_count * beam_width // (cluster_count * groups))
    positions = jnp.arange(capacity, dtype=jnp.int32)
    dispatch = (membership.T[:, None, :] == 1) & (
        slot_index.T[:, None, :] == positions[None, :, None]
    )
    picked = jnp.einsum(
        "csq,qd->csd",
        dispatch.astype(jnp.bfloat16),
        query_block,
        preferred_element_type=jnp.float32,
    ).astype(jnp.bfloat16)
    slot_centroid = jnp.sum(jnp.where(dispatch, cscore.T[:, None, :], 0.0), axis=2)
    logits = (
        jnp.einsum("csd,cjd->csj", picked, leaves, preferred_element_type=jnp.float32) * score_scale
    )
    logits = logits + slot_centroid[:, :, None]
    slot_max = jnp.max(logits, axis=2)
    weights = jnp.exp(logits - slot_max[:, :, None])
    slot_sum = jnp.sum(weights, axis=2)
    slot_accum = jnp.einsum(
        "csj,cjd->csd", weights.astype(jnp.bfloat16), leaves, preferred_element_type=jnp.float32
    )
    slot_total = cluster_count * capacity
    dispatch_flat = dispatch.reshape(slot_total, query_count)
    slot_max_flat = slot_max.reshape(slot_total)
    masked_max = jnp.where(dispatch_flat, slot_max_flat[:, None], floor_value)
    lmax_part = jnp.max(masked_max, axis=0)
    exponent = jnp.where(dispatch_flat, slot_max_flat[:, None] - lmax_part[None, :], 0.0)
    factors = jnp.where(dispatch_flat, jnp.exp(exponent), 0.0)
    lsum_part = jnp.sum(factors * slot_sum.reshape(slot_total)[:, None], axis=0)
    accum_part = jnp.dot(
        factors.T,
        slot_accum.reshape(slot_total, model_width),
        precision=lax.Precision.HIGHEST,
        preferred_element_type=jnp.float32,
    )
    state = (cmax_part, csum_part, beam_part, lmax_part, lsum_part, accum_part)
    row_count = query_count // groups
    merged = merged_2(state, "cluster", combine_states)
    row_start = lax.axis_index("cluster") * row_count
    own = tuple((lax.dynamic_slice_in_dim(member, row_start, row_count, 0) for member in merged))
    cmax_own, csum_own, beam_own, lmax_own, lsum_own, accum_own = own
    lse = cmax_own + jnp.log(csum_own)
    beam_logprob = beam_own - lse[:, None]
    readout = (accum_own / lsum_own[:, None]).astype(jnp.bfloat16)
    return (readout, beam_logprob)


MESH = pl.DeviceIdType.MESH
CODE_MAX = 32767.0
LANES = 128


def fused_kernel(
    groups,
    capacity,
    q_ref,
    cent_ref,
    leaves_ref,
    beam_ref,
    readout_ref,
    logprob_ref,
    block,
    cent_buf,
    beam_buf,
    leaf_buf,
    partial_buf,
    weight_buf,
    centroid_send,
    centroid_recv,
    held_buf,
    near_recv,
    level_buf,
    near_level,
    stat_send,
    stat_recv,
    code_send,
    code_recv,
    leaf_sem,
    own_sem,
    q_send_sem,
    q_recv_sem,
    centroid_send_sem,
    centroid_recv_sem,
    near_send_sem,
    near_recv_sem,
    stat_send_sem,
    stat_recv_sem,
    code_send_sem,
    code_recv_sem,
):
    rows, width = q_ref.shape
    clusters = cent_ref.shape[0]
    total = groups * rows
    beam_width = beam_ref.shape[0]
    chips = groups // 2
    half = width // 2
    score_scale = 1.0 / math.sqrt(width)
    f32 = jnp.float32
    me = lax.axis_index("cluster")
    chip, core = me // 2, me % 2
    sibling = chip * 2 + (1 - core)
    first = me * clusters

    def peer_at(offset, side):
        return lax.rem(chip + offset, chips) * 2 + side

    peers = [peer_at(o, s) for o in range(1, chips) for s in (core, 1 - core)] + [sibling]

    def signal_peers():
        barrier = pltpu.get_barrier_semaphore()
        for peer in peers:
            pl.semaphore_signal(barrier, inc=1, device_id={"cluster": peer}, device_id_type=MESH)
        pl.semaphore_wait(barrier, len(peers))

    own_copies = [
        pltpu.make_async_copy(q_ref.at[:, h * half : (h + 1) * half], block.at[h, me], own_sem.at[h])
        for h in range(2)
    ] + [
        pltpu.make_async_copy(beam_ref, beam_buf, own_sem.at[2]),
        pltpu.make_async_copy(cent_ref, cent_buf, own_sem.at[3]),
    ]
    leaf_copies = [
        pltpu.make_async_copy(leaves_ref.at[c], leaf_buf.at[c], leaf_sem.at[c])
        for c in range(clusters)
    ]
    for copy in own_copies + leaf_copies:
        copy.start()
    signal_peers()

    def push(src, dst, send_sem, recv_sem, peer):
        return pltpu.make_async_remote_copy(
            src_ref=src,
            dst_ref=dst,
            send_sem=send_sem,
            recv_sem=recv_sem,
            device_id={"cluster": peer},
            device_id_type=MESH,
        )

    sends = []
    for h in range(2):
        own_copies[h].wait()
        mine = block.at[h, me]
        for number, offset in enumerate(range(1, chips)):
            peer = peer_at(offset, core)
            sends.append(push(mine, mine, q_send_sem.at[h, number], q_recv_sem.at[h, me], peer))
            sends[-1].start()
        sends.append(
            push(mine, mine, q_send_sem.at[h, chips - 1], q_recv_sem.at[h, me], sibling)
        )
        sends[-1].start()

    own_copies[2].wait()
    beams = beam_buf[...]
    members = jnp.concatenate(
        [
            jnp.max((beams == first + c).astype(f32), axis=0, keepdims=True)
            for c in range(clusters)
        ],
        axis=0,
    )
    upper = (
        lax.broadcasted_iota(jnp.int32, (total, total), 0)
        <= lax.broadcasted_iota(jnp.int32, (total, total), 1)
    ).astype(jnp.bfloat16)
    padded = jnp.concatenate([members, jnp.zeros((LANES - clusters, total), f32)], axis=0)
    counts = jnp.dot(padded.astype(jnp.bfloat16), upper, preferred_element_type=f32)
    slots = jnp.where(padded > 0.0, counts, 0.0)
    slot_number = lax.broadcasted_iota(jnp.int32, (capacity, total), 0).astype(f32) + 1.0
    dispatch = jnp.concatenate(
        [(slots[c : c + 1, :] == slot_number).astype(f32) for c in range(clusters)], axis=0
    )
    slot_total = clusters * capacity
    slots_down = slots.T
    slot_across = lax.broadcasted_iota(jnp.int32, (total, slot_total), 1)
    wanted = jnp.concatenate(
        [jnp.broadcast_to(slots_down[:, c : c + 1], (total, capacity)) for c in range(clusters)],
        axis=1,
    )
    collect = (wanted == (slot_across % capacity).astype(f32) + 1.0).astype(jnp.bfloat16)

    def arrival(h, origin):
        place = block.at[h, origin]
        return push(place, place, q_send_sem.at[h, 0], q_recv_sem.at[h, origin], sibling)

    def relay_half(h):
        for offset in range(1, chips):
            origin = peer_at(chips - offset, core)
            arrival(h, origin).wait_recv()
            place = block.at[h, origin]
            relay = push(
                place,
                place,
                q_send_sem.at[h, chips - 1 + offset],
                q_recv_sem.at[h, origin],
                sibling,
            )
            relay.start()
            sends.append(relay)

    def finish_half(h):
        arrival(h, sibling).wait_recv()
        for offset in range(1, chips):
            arrival(h, peer_at(chips - offset, 1 - core)).wait_recv()
        return block[h].reshape(total, half)

    nt = (((1,), (1,)), ((), ()))
    dispatch_low = dispatch.astype(jnp.bfloat16)

    def pick(rows_of):
        return jnp.dot(dispatch_low, rows_of, preferred_element_type=f32).astype(jnp.bfloat16)

    def scores(picked, c, h):
        return lax.dot_general(
            picked[c * capacity : (c + 1) * capacity],
            leaf_buf[c, :, h * half : (h + 1) * half],
            nt,
            preferred_element_type=f32,
        )

    relay_half(0)
    queries_low = finish_half(0)
    picked_low = pick(queries_low)
    for c in range(clusters // 2):
        leaf_copies[c].wait()
    for c in range(clusters // 2):
        partial_buf[c] = scores(picked_low, c, 0)
    relay_half(1)
    for c in range(clusters // 2, clusters):
        leaf_copies[c].wait()
    for c in range(clusters // 2, clusters):
        partial_buf[c] = scores(picked_low, c, 0)
    own_copies[3].wait()
    queries_high = finish_half(1)
    cent = jnp.concatenate(
        [cent_buf[...], jnp.zeros((LANES - clusters, width), cent_buf.dtype)], axis=0
    )
    cscore = (
        lax.dot_general(cent[:, 0:half], queries_low, nt, preferred_element_type=f32)
        + lax.dot_general(cent[:, half:], queries_high, nt, preferred_element_type=f32)
    )[0:clusters]
    cscore = cscore * score_scale
    part_max = jnp.max(cscore, axis=0, keepdims=True)
    part_sum = jnp.sum(jnp.exp(cscore - part_max), axis=0, keepdims=True)
    picks = sum(
        jnp.where(beams == first + c, cscore[c : c + 1, :], 0.0) for c in range(clusters)
    )
    for g in range(groups):
        lanes = slice(g * rows, (g + 1) * rows)
        centroid_send[g, 0:beam_width, 0:rows] = picks[:, lanes]
        centroid_send[g, beam_width : beam_width + 1, 0:rows] = part_max[:, lanes]
        centroid_send[g, beam_width + 1 : beam_width + 2, 0:rows] = part_sum[:, lanes]
    centroid_copies = [
        push(
            centroid_send.at[peer],
            centroid_recv.at[me],
            centroid_send_sem.at[number],
            centroid_recv_sem.at[me],
            peer,
        )
        for number, peer in enumerate(peers)
    ]
    for copy in centroid_copies:
        copy.start()

    picked_high = pick(queries_high)
    lane = lax.broadcasted_iota(jnp.int32, (slot_total, LANES), 1)
    owner = lax.broadcasted_iota(jnp.int32, (slot_total, LANES), 0) // capacity
    slot_scores = (
        lax.dot_general(picked_low, cent[:, 0:half], nt, preferred_element_type=f32)
        + lax.dot_general(picked_high, cent[:, half:], nt, preferred_element_type=f32)
    ) * score_scale
    slot_centroid = jnp.sum(jnp.where(lane == owner, slot_scores, 0.0), axis=1, keepdims=True)

    def weigh(c, h):
        return jnp.dot(
            weight_buf[c],
            leaf_buf[c, :, h * half : (h + 1) * half],
            preferred_element_type=f32,
        )

    peaks, masses, sums = [], [], []
    current = partial_buf[0] + scores(picked_high, 0, 1)
    for c in range(clusters):
        upcoming = None
        if c + 1 < clusters:
            upcoming = partial_buf[c + 1] + scores(picked_high, c + 1, 1)
        peak = jnp.max(current, axis=1, keepdims=True)
        weights = jnp.exp((current - peak) * score_scale)
        masses.append(jnp.sum(weights, axis=1, keepdims=True))
        peaks.append(peak)
        weight_buf[c] = weights.astype(jnp.bfloat16)
        sums.append(weigh(c, 0))
        current = upcoming
    level = jnp.concatenate(peaks, axis=0) * score_scale + slot_centroid
    mass = jnp.concatenate(masses, axis=0)

    used = dispatch > 0.0
    top = jnp.max(jnp.where(used, level, floor_value), axis=0, keepdims=True)
    slot_top = jnp.max(jnp.where(used, top, floor_value), axis=1, keepdims=True)
    filled = jnp.max(dispatch, axis=1, keepdims=True) > 0.0
    gain = jnp.where(filled, jnp.exp(jnp.where(filled, level - slot_top, 0.0)), 0.0)
    denom = jnp.sum(jnp.where(used, mass * gain, 0.0), axis=0, keepdims=True)
    for g in range(groups):
        lanes = slice(g * rows, (g + 1) * rows)
        level_buf[g % 2, g // 2, 0:1, 0:rows] = top[:, lanes]
        level_buf[g % 2, g // 2, 1:2, 0:rows] = denom[:, lanes]
    order = [2, 1, 3, 0] if chips == 4 else list(range(1, chips)) + [0]
    level_copy = push(
        level_buf.at[1 - core],
        near_level,
        near_send_sem.at[0, chips],
        near_recv_sem.at[0, chips],
        sibling,
    )
    level_copy.start()
    near_copies = [level_copy]

    def near_copy(h, offset):
        g = lax.rem(chip + offset, chips)
        return push(
            held_buf.at[h, 1 - core, g],
            near_recv.at[h, g],
            near_send_sem.at[h, offset],
            near_recv_sem.at[h, g],
            sibling,
        )

    def share_half(h, sums):
        scaled = jnp.concatenate(sums, axis=0) * gain
        coarse = scaled.astype(jnp.bfloat16)
        fine = (scaled - coarse.astype(f32)).astype(jnp.bfloat16)
        held = jnp.dot(collect, coarse, preferred_element_type=f32) + jnp.dot(
            collect, fine, preferred_element_type=f32
        )
        for g in range(groups):
            held_buf[h, g % 2, g // 2] = held[g * rows : (g + 1) * rows]
        for offset in order:
            near_copies.append(near_copy(h, offset))
            near_copies[-1].start()

    diagonal = lax.broadcasted_iota(jnp.int32, (rows, LANES), 0) == lax.broadcasted_iota(
        jnp.int32, (rows, LANES), 1
    )

    def to_column(row):
        return jnp.sum(jnp.where(diagonal, row, 0.0), axis=1, keepdims=True)

    def to_row(column):
        return jnp.sum(jnp.where(diagonal, column, 0.0), axis=0, keepdims=True)

    result_copies = []

    def chip_levels():
        level_copy.wait_recv()
        found = []
        for offset in order:
            g = lax.rem(chip + offset, chips)
            here, near = level_buf[core, g], near_level[g]
            high = jnp.maximum(here[0:1], near[0:1])
            here_gain, near_gain = jnp.exp(here[0:1] - high), jnp.exp(near[0:1] - high)
            amount = here[1:2] * here_gain + near[1:2] * near_gain
            found.append((high, amount, to_column(here_gain), to_column(near_gain)))
        return found

    def merge_half(h, levels):
        for number, offset in enumerate(order):
            g = lax.rem(chip + offset, chips)
            high, amount, here_gain, near_gain = levels[number]
            near_copy(h, offset).wait_recv()
            both = held_buf[h, core, g] * here_gain + near_recv[h, g] * near_gain
            if offset == 0:
                return both
            largest = jnp.maximum(jnp.max(jnp.abs(both), axis=1, keepdims=True), 1e-30)
            code_send[h, number] = (
                jnp.round(both * (CODE_MAX / largest)).astype(jnp.int32).astype(jnp.int16)
            )
            stat_send[h, number, 0:1] = high
            stat_send[h, number, 1:2] = amount
            stat_send[h, number, 2:3] = to_row(largest * (1.0 / CODE_MAX))
            peer = g * 2 + core
            for source, target, send_sem, recv_sem in (
                (stat_send, stat_recv, stat_send_sem, stat_recv_sem),
                (code_send, code_recv, code_send_sem, code_recv_sem),
            ):
                copy = push(
                    source.at[h, number],
                    target.at[h, chip],
                    send_sem.at[h, number],
                    recv_sem.at[h, chip],
                    peer,
                )
                copy.start()
                result_copies.append(copy)

    share_half(0, sums)
    sums_high = [weigh(c, 1) for c in range(clusters // 2)]
    levels = chip_levels()
    own_low = merge_half(0, levels)
    sums_high += [weigh(c, 1) for c in range(clusters // 2, clusters)]
    share_half(1, sums_high)
    own_high_half = merge_half(1, levels)
    own_top, own_amount = levels[-1][0], levels[-1][1]

    for number, peer in enumerate(peers):
        push(
            centroid_send.at[peer],
            centroid_recv.at[peer],
            centroid_send_sem.at[number],
            centroid_recv_sem.at[peer],
            peer,
        ).wait_recv()
    centroid_recv[me] = centroid_send[me]
    parts = [centroid_recv[g] for g in range(groups)]
    cmax = functools.reduce(jnp.maximum, [p[beam_width : beam_width + 1] for p in parts])
    csum = sum(
        p[beam_width + 1 : beam_width + 2] * jnp.exp(p[beam_width : beam_width + 1] - cmax)
        for p in parts
    )
    logprob = sum(p[0:beam_width] for p in parts) - (cmax + jnp.log(csum))
    logprob_ref[...] = logprob[:, 0:rows]

    sources = [lax.rem(chip + offset, chips) for offset in range(1, chips)]
    own_share = whole = None
    for h, own in enumerate((own_low, own_high_half)):
        for g in sources:
            push(
                stat_send.at[h, 0],
                stat_recv.at[h, g],
                stat_send_sem.at[h, 0],
                stat_recv_sem.at[h, g],
                sibling,
            ).wait_recv()
        stats = [stat_recv[h, g] for g in sources]
        if h == 0:
            overall = functools.reduce(jnp.maximum, [t[0:1] for t in stats], own_top)
            own_share = jnp.exp(own_top - overall)
            shares = [jnp.exp(t[0:1] - overall) for t in stats]
            whole = own_amount * own_share + sum(f * t[1:2] for f, t in zip(shares, stats))
        merged = own * to_column(own_share / whole)
        for g, share, stat in zip(sources, shares, stats):
            push(
                code_send.at[h, 0],
                code_recv.at[h, g],
                code_send_sem.at[h, 0],
                code_recv_sem.at[h, g],
                sibling,
            ).wait_recv()
            merged = merged + code_recv[h, g].astype(jnp.int32).astype(f32) * to_column(
                share * stat[2:3] / whole
            )
        readout_ref[:, h * half : (h + 1) * half] = merged.astype(jnp.bfloat16)

    for copy in sends + centroid_copies + near_copies + result_copies:
        copy.wait_send()


def store_kernel(readout_ref, logprob_ref, readout_out, logprob_out, sems):
    copies = [
        pltpu.make_async_copy(readout_ref, readout_out, sems.at[0]),
        pltpu.make_async_copy(logprob_ref, logprob_out, sems.at[1]),
    ]
    for copy in copies:
        copy.start()
    for copy in copies:
        copy.wait()


def fused(queries, centroids, leaves, beam):
    groups = lax.axis_size("cluster")
    rows, width = queries.shape
    clusters = centroids.shape[0]
    total, beam_width = beam.shape
    capacity = 2 * total * beam_width // (clusters * groups)
    if rows % 16 or capacity % 16 or groups % 2 or groups > 16 or rows > LANES or beam_width != 8 or width % 256:
        return per_device(queries, centroids, leaves, beam)
    vmem = pl.BlockSpec(memory_space=pltpu.VMEM)
    hbm = pl.BlockSpec(memory_space=pltpu.HBM)
    dma = pltpu.SemaphoreType.DMA
    peers = groups - 1
    chips = groups // 2
    half = width // 2
    readout, logprob = pl.pallas_call(
        functools.partial(fused_kernel, groups, capacity),
        out_shape=(
            jax.ShapeDtypeStruct((rows, width), jnp.bfloat16),
            jax.ShapeDtypeStruct((beam_width, rows), jnp.float32),
        ),
        in_specs=[hbm, hbm, hbm, hbm],
        out_specs=(vmem, vmem),
        scratch_shapes=[
            pltpu.VMEM((2, groups, rows, half), jnp.bfloat16),
            pltpu.VMEM(centroids.shape, jnp.bfloat16),
            pltpu.VMEM((beam_width, total), jnp.int32),
            pltpu.VMEM(leaves.shape, jnp.bfloat16),
            pltpu.VMEM((clusters, capacity, leaves.shape[1]), jnp.float32),
            pltpu.VMEM((clusters, capacity, leaves.shape[1]), jnp.bfloat16),
            pltpu.VMEM((groups, beam_width + 8, LANES), jnp.float32),
            pltpu.VMEM((groups, beam_width + 8, LANES), jnp.float32),
            pltpu.VMEM((2, 2, chips, rows, half), jnp.float32),
            pltpu.VMEM((2, chips, rows, half), jnp.float32),
            pltpu.VMEM((2, chips, 8, LANES), jnp.float32),
            pltpu.VMEM((chips, 8, LANES), jnp.float32),
            pltpu.VMEM((2, chips, 8, LANES), jnp.float32),
            pltpu.VMEM((2, chips, 8, LANES), jnp.float32),
            pltpu.VMEM((2, chips, rows, half), jnp.int16),
            pltpu.VMEM((2, chips, rows, half), jnp.int16),
            dma((clusters,)),
            dma((4,)),
            dma((2, groups)),
            dma((2, groups)),
            dma((peers,)),
            dma((groups,)),
            dma((2, chips + 1)),
            dma((2, chips + 1)),
            dma((2, chips)),
            dma((2, chips)),
            dma((2, chips)),
            dma((2, chips)),
        ],
        compiler_params=pltpu.CompilerParams(
            collective_id=0, has_side_effects=True, vmem_limit_bytes=64 * 1024 * 1024
        ),
    )(queries, centroids, leaves, beam.T)
    readout, logprob = pl.pallas_call(
        store_kernel,
        out_shape=(
            jax.ShapeDtypeStruct(readout.shape, readout.dtype),
            jax.ShapeDtypeStruct(logprob.shape, logprob.dtype),
        ),
        in_specs=[hbm, hbm],
        out_specs=(hbm, hbm),
        scratch_shapes=[dma((2,))],
        compiler_params=pltpu.CompilerParams(vmem_limit_bytes=64 * 1024 * 1024),
    )(readout, logprob)
    return readout, logprob.T


def solution(mesh):
    return jax.shard_map(
        fused,
        mesh=mesh,
        in_specs=(
            P(("query", "cluster"), None),
            P("cluster", None),
            P("cluster", None, None),
            P("query", None),
        ),
        out_specs=(P(("query", "cluster"), None), P(("query", "cluster"), None)),
        check_vma=False,
    )
```

```python
import functools
import math

import jax
import jax.numpy as jnp
from jax import lax
from jax.experimental import pallas as pl
from jax.experimental.pallas import tpu as pltpu
from jax.sharding import PartitionSpec as P

floor_value = -1e30


def merged_2(part, axis, combine):
    gathered = jax.tree.map(lambda a: lax.all_gather(a, axis), part)

    def take(source):
        return jax.tree.map(lambda a: lax.dynamic_index_in_dim(a, source, 0, False), gathered)

    return lax.fori_loop(
        1, lax.axis_size(axis), lambda source, state: combine(state, take(source)), take(0)
    )


def combine_states(first, second):
    cmax_one, csum_one, beam_one, lmax_one, lsum_one, accum_one = first
    cmax_two, csum_two, beam_two, lmax_two, lsum_two, accum_two = second
    cmax_new = jnp.maximum(cmax_one, cmax_two)
    csum_new = csum_one * jnp.exp(cmax_one - cmax_new) + csum_two * jnp.exp(cmax_two - cmax_new)
    lmax_new = jnp.maximum(lmax_one, lmax_two)
    factor_one = jnp.exp(lmax_one - lmax_new)
    factor_two = jnp.exp(lmax_two - lmax_new)
    lsum_new = lsum_one * factor_one + lsum_two * factor_two
    accum_new = accum_one * factor_one[:, None] + accum_two * factor_two[:, None]
    return (cmax_new, csum_new, beam_one + beam_two, lmax_new, lsum_new, accum_new)


def per_device(queries, centroids, leaves, beam):
    groups = lax.axis_size("cluster")
    query_block = lax.all_gather(queries, "cluster", axis=0, tiled=True)
    query_count, model_width = query_block.shape
    cluster_count, leaf_count, unused_width = leaves.shape
    beam_width = beam.shape[1]
    score_scale = 1.0 / math.sqrt(model_width)
    first_cluster = lax.axis_index("cluster") * cluster_count
    cscore = jnp.dot(query_block, centroids.T, preferred_element_type=jnp.float32) * score_scale
    cmax_part = jnp.max(cscore, axis=1)
    csum_part = jnp.sum(jnp.exp(cscore - cmax_part[:, None]), axis=1)
    owned = first_cluster + jnp.arange(cluster_count, dtype=jnp.int32)
    matches = beam[:, :, None] == owned[None, None, :]
    beam_part = jnp.sum(jnp.where(matches, cscore[:, None, :], 0.0), axis=2)
    membership = jnp.any(matches, axis=1).astype(jnp.int32)
    slot_index = jnp.cumsum(membership, axis=0) - 1
    capacity = max(4, 2 * query_count * beam_width // (cluster_count * groups))
    positions = jnp.arange(capacity, dtype=jnp.int32)
    dispatch = (membership.T[:, None, :] == 1) & (
        slot_index.T[:, None, :] == positions[None, :, None]
    )
    picked = jnp.einsum(
        "csq,qd->csd",
        dispatch.astype(jnp.bfloat16),
        query_block,
        preferred_element_type=jnp.float32,
    ).astype(jnp.bfloat16)
    slot_centroid = jnp.sum(jnp.where(dispatch, cscore.T[:, None, :], 0.0), axis=2)
    logits = (
        jnp.einsum("csd,cjd->csj", picked, leaves, preferred_element_type=jnp.float32) * score_scale
    )
    logits = logits + slot_centroid[:, :, None]
    slot_max = jnp.max(logits, axis=2)
    weights = jnp.exp(logits - slot_max[:, :, None])
    slot_sum = jnp.sum(weights, axis=2)
    slot_accum = jnp.einsum(
        "csj,cjd->csd", weights.astype(jnp.bfloat16), leaves, preferred_element_type=jnp.float32
    )
    slot_total = cluster_count * capacity
    dispatch_flat = dispatch.reshape(slot_total, query_count)
    slot_max_flat = slot_max.reshape(slot_total)
    masked_max = jnp.where(dispatch_flat, slot_max_flat[:, None], floor_value)
    lmax_part = jnp.max(masked_max, axis=0)
    exponent = jnp.where(dispatch_flat, slot_max_flat[:, None] - lmax_part[None, :], 0.0)
    factors = jnp.where(dispatch_flat, jnp.exp(exponent), 0.0)
    lsum_part = jnp.sum(factors * slot_sum.reshape(slot_total)[:, None], axis=0)
    accum_part = jnp.dot(
        factors.T,
        slot_accum.reshape(slot_total, model_width),
        precision=lax.Precision.HIGHEST,
        preferred_element_type=jnp.float32,
    )
    state = (cmax_part, csum_part, beam_part, lmax_part, lsum_part, accum_part)
    row_count = query_count // groups
    merged = merged_2(state, "cluster", combine_states)
    row_start = lax.axis_index("cluster") * row_count
    own = tuple((lax.dynamic_slice_in_dim(member, row_start, row_count, 0) for member in merged))
    cmax_own, csum_own, beam_own, lmax_own, lsum_own, accum_own = own
    lse = cmax_own + jnp.log(csum_own)
    beam_logprob = beam_own - lse[:, None]
    readout = (accum_own / lsum_own[:, None]).astype(jnp.bfloat16)
    return (readout, beam_logprob)


MESH = pl.DeviceIdType.MESH
CODE_MAX = 32767.0
LANES = 128


def fused_kernel(
    groups,
    capacity,
    q_ref,
    cent_ref,
    leaves_ref,
    beam_ref,
    readout_ref,
    logprob_ref,
    block,
    cent_buf,
    beam_buf,
    leaf_buf,
    centroid_send,
    centroid_recv,
    held_buf,
    near_recv,
    level_buf,
    near_level,
    stat_send,
    stat_recv,
    code_send,
    code_recv,
    leaf_sem,
    own_sem,
    q_send_sem,
    q_recv_sem,
    centroid_send_sem,
    centroid_recv_sem,
    near_send_sem,
    near_recv_sem,
    stat_send_sem,
    stat_recv_sem,
    code_send_sem,
    code_recv_sem,
):
    rows, width = q_ref.shape
    clusters = cent_ref.shape[0]
    total = groups * rows
    beam_width = beam_ref.shape[0]
    chips = groups // 2
    score_scale = 1.0 / math.sqrt(width)
    f32 = jnp.float32
    me = lax.axis_index("cluster")
    chip, core = me // 2, me % 2
    sibling = chip * 2 + (1 - core)
    first = me * clusters

    def peer_at(offset, side):
        return lax.rem(chip + offset, chips) * 2 + side

    peers = [peer_at(o, s) for o in range(1, chips) for s in (core, 1 - core)] + [sibling]

    def signal_peers():
        barrier = pltpu.get_barrier_semaphore()
        for peer in peers:
            pl.semaphore_signal(barrier, inc=1, device_id={"cluster": peer}, device_id_type=MESH)
        pl.semaphore_wait(barrier, len(peers))

    own_copies = [
        pltpu.make_async_copy(q_ref, block.at[me], own_sem.at[0]),
        pltpu.make_async_copy(beam_ref, beam_buf, own_sem.at[1]),
        pltpu.make_async_copy(cent_ref, cent_buf, own_sem.at[2]),
    ]
    leaf_copies = [
        pltpu.make_async_copy(leaves_ref.at[c], leaf_buf.at[c], leaf_sem.at[c])
        for c in range(clusters)
    ]
    for copy in own_copies + leaf_copies:
        copy.start()
    signal_peers()

    def push(src, dst, send_sem, recv_sem, peer):
        return pltpu.make_async_remote_copy(
            src_ref=src,
            dst_ref=dst,
            send_sem=send_sem,
            recv_sem=recv_sem,
            device_id={"cluster": peer},
            device_id_type=MESH,
        )

    own_copies[0].wait()
    mine = block.at[me]
    sends = []
    for number, offset in enumerate(range(1, chips)):
        peer = peer_at(offset, core)
        sends.append(push(mine, mine, q_send_sem.at[number], q_recv_sem.at[me], peer))
    sends.append(push(mine, mine, q_send_sem.at[chips - 1], q_recv_sem.at[me], sibling))
    for copy in sends:
        copy.start()

    own_copies[1].wait()
    beams = beam_buf[...]
    members = jnp.concatenate(
        [
            jnp.max((beams == first + c).astype(f32), axis=0, keepdims=True)
            for c in range(clusters)
        ],
        axis=0,
    )
    upper = (
        lax.broadcasted_iota(jnp.int32, (total, total), 0)
        <= lax.broadcasted_iota(jnp.int32, (total, total), 1)
    ).astype(jnp.bfloat16)
    padded = jnp.concatenate([members, jnp.zeros((LANES - clusters, total), f32)], axis=0)
    counts = jnp.dot(padded.astype(jnp.bfloat16), upper, preferred_element_type=f32)
    slots = jnp.where(padded > 0.0, counts, 0.0)
    slot_number = lax.broadcasted_iota(jnp.int32, (capacity, total), 0).astype(f32) + 1.0
    dispatch = jnp.concatenate(
        [(slots[c : c + 1, :] == slot_number).astype(f32) for c in range(clusters)], axis=0
    )
    slot_total = clusters * capacity
    slots_down = slots.T
    slot_across = lax.broadcasted_iota(jnp.int32, (total, slot_total), 1)
    wanted = jnp.concatenate(
        [jnp.broadcast_to(slots_down[:, c : c + 1], (total, capacity)) for c in range(clusters)],
        axis=1,
    )
    collect = (wanted == (slot_across % capacity).astype(f32) + 1.0).astype(jnp.bfloat16)

    def arrival(origin):
        return push(block.at[origin], block.at[origin], q_send_sem.at[0], q_recv_sem.at[origin], sibling)

    for offset in range(1, chips):
        origin = peer_at(chips - offset, core)
        arrival(origin).wait_recv()
        relay = push(
            block.at[origin],
            block.at[origin],
            q_send_sem.at[chips - 1 + offset],
            q_recv_sem.at[origin],
            sibling,
        )
        relay.start()
        sends.append(relay)
    arrival(sibling).wait_recv()
    for offset in range(1, chips):
        arrival(peer_at(chips - offset, 1 - core)).wait_recv()
    own_copies[2].wait()

    queries = block[...].reshape(total, width)
    cent = jnp.concatenate(
        [cent_buf[...], jnp.zeros((LANES - clusters, width), cent_buf.dtype)], axis=0
    )
    nt = (((1,), (1,)), ((), ()))
    cscore = lax.dot_general(cent, queries, nt, preferred_element_type=f32)[0:clusters]
    cscore = cscore * score_scale
    part_max = jnp.max(cscore, axis=0, keepdims=True)
    part_sum = jnp.sum(jnp.exp(cscore - part_max), axis=0, keepdims=True)
    picks = sum(
        jnp.where(beams == first + c, cscore[c : c + 1, :], 0.0) for c in range(clusters)
    )
    for g in range(groups):
        lanes = slice(g * rows, (g + 1) * rows)
        centroid_send[g, 0:beam_width, 0:rows] = picks[:, lanes]
        centroid_send[g, beam_width : beam_width + 1, 0:rows] = part_max[:, lanes]
        centroid_send[g, beam_width + 1 : beam_width + 2, 0:rows] = part_sum[:, lanes]
    centroid_copies = [
        push(
            centroid_send.at[peer],
            centroid_recv.at[me],
            centroid_send_sem.at[number],
            centroid_recv_sem.at[me],
            peer,
        )
        for number, peer in enumerate(peers)
    ]
    for copy in centroid_copies:
        copy.start()

    picked = jnp.dot(
        dispatch.astype(jnp.bfloat16), queries, preferred_element_type=f32
    ).astype(jnp.bfloat16)
    lane = lax.broadcasted_iota(jnp.int32, (slot_total, LANES), 1)
    owner = lax.broadcasted_iota(jnp.int32, (slot_total, LANES), 0) // capacity
    slot_scores = lax.dot_general(picked, cent, nt, preferred_element_type=f32) * score_scale
    slot_centroid = jnp.sum(jnp.where(lane == owner, slot_scores, 0.0), axis=1, keepdims=True)
    for copy in leaf_copies:
        copy.wait()

    def scores(c):
        return lax.dot_general(
            leaf_buf[c],
            picked[c * capacity : (c + 1) * capacity],
            nt,
            preferred_element_type=f32,
        )

    slot_diagonal = lax.broadcasted_iota(
        jnp.int32, (capacity, capacity), 0
    ) == lax.broadcasted_iota(jnp.int32, (capacity, capacity), 1)

    def slot_column(row):
        return jnp.sum(jnp.where(slot_diagonal, row, 0.0), axis=1, keepdims=True)

    peaks, masses, sums = [], [], []
    current = scores(0)
    for c in range(clusters):
        upcoming = scores(c + 1) if c + 1 < clusters else None
        peak = jnp.max(current, axis=0, keepdims=True)
        weights = jnp.exp((current - peak) * score_scale)
        masses.append(slot_column(jnp.sum(weights, axis=0, keepdims=True)))
        peaks.append(slot_column(peak))
        sums.append(
            lax.dot_general(
                weights.astype(jnp.bfloat16),
                leaf_buf[c],
                (((0,), (0,)), ((), ())),
                preferred_element_type=f32,
            )
        )
        current = upcoming
    level = jnp.concatenate(peaks, axis=0) * score_scale + slot_centroid
    mass = jnp.concatenate(masses, axis=0)
    summed = jnp.concatenate(sums, axis=0)

    used = dispatch > 0.0
    top = jnp.max(jnp.where(used, level, floor_value), axis=0, keepdims=True)
    slot_top = jnp.max(jnp.where(used, top, floor_value), axis=1, keepdims=True)
    filled = jnp.max(dispatch, axis=1, keepdims=True) > 0.0
    gain = jnp.where(filled, jnp.exp(jnp.where(filled, level - slot_top, 0.0)), 0.0)
    denom = jnp.sum(jnp.where(used, mass * gain, 0.0), axis=0, keepdims=True)
    scaled = summed * gain
    coarse = scaled.astype(jnp.bfloat16)
    fine = (scaled - coarse.astype(f32)).astype(jnp.bfloat16)
    held = jnp.dot(collect, coarse, preferred_element_type=f32) + jnp.dot(
        collect, fine, preferred_element_type=f32
    )
    for g in range(groups):
        lanes = slice(g * rows, (g + 1) * rows)
        level_buf[g % 2, g // 2, 0:1, 0:rows] = top[:, lanes]
        level_buf[g % 2, g // 2, 1:2, 0:rows] = denom[:, lanes]
        held_buf[g % 2, g // 2] = held[lanes]
    order = [2, 1, 3, 0] if chips == 4 else list(range(1, chips)) + [0]
    near_copies = [
        push(
            level_buf.at[1 - core],
            near_level,
            near_send_sem.at[chips],
            near_recv_sem.at[chips],
            sibling,
        )
    ]
    for offset in order:
        g = lax.rem(chip + offset, chips)
        near_copies.append(
            push(
                held_buf.at[1 - core, g],
                near_recv.at[g],
                near_send_sem.at[offset],
                near_recv_sem.at[g],
                sibling,
            )
        )
    for copy in near_copies:
        copy.start()

    near_copies[0].wait_recv()
    diagonal = lax.broadcasted_iota(jnp.int32, (rows, LANES), 0) == lax.broadcasted_iota(
        jnp.int32, (rows, LANES), 1
    )

    def to_column(row):
        return jnp.sum(jnp.where(diagonal, row, 0.0), axis=1, keepdims=True)

    def to_row(column):
        return jnp.sum(jnp.where(diagonal, column, 0.0), axis=0, keepdims=True)

    result_copies = []
    for number, offset in enumerate(order):
        g = lax.rem(chip + offset, chips)
        here, near = level_buf[core, g], near_level[g]
        high = jnp.maximum(here[0:1], near[0:1])
        here_gain, near_gain = jnp.exp(here[0:1] - high), jnp.exp(near[0:1] - high)
        amount = here[1:2] * here_gain + near[1:2] * near_gain
        push(
            held_buf.at[1 - core, g],
            near_recv.at[g],
            near_send_sem.at[offset],
            near_recv_sem.at[g],
            sibling,
        ).wait_recv()
        both = held_buf[core, g] * to_column(here_gain) + near_recv[g] * to_column(near_gain)
        if offset == 0:
            own_high, own_amount, own_both = high, amount, both
            continue
        largest = jnp.maximum(jnp.max(jnp.abs(both), axis=1, keepdims=True), 1e-30)
        code_send[number] = (
            jnp.round(both * (CODE_MAX / largest)).astype(jnp.int32).astype(jnp.int16)
        )
        stat_send[number, 0:1] = high
        stat_send[number, 1:2] = amount
        stat_send[number, 2:3] = to_row(largest * (1.0 / CODE_MAX))
        peer = g * 2 + core
        for buffers, sems in (
            ((stat_send, stat_recv), (stat_send_sem, stat_recv_sem)),
            ((code_send, code_recv), (code_send_sem, code_recv_sem)),
        ):
            copy = push(
                buffers[0].at[number], buffers[1].at[chip], sems[0].at[number], sems[1].at[chip], peer
            )
            copy.start()
            result_copies.append(copy)

    for number, peer in enumerate(peers):
        push(
            centroid_send.at[peer],
            centroid_recv.at[peer],
            centroid_send_sem.at[number],
            centroid_recv_sem.at[peer],
            peer,
        ).wait_recv()
    centroid_recv[me] = centroid_send[me]
    parts = [centroid_recv[g] for g in range(groups)]
    cmax = functools.reduce(jnp.maximum, [p[beam_width : beam_width + 1] for p in parts])
    csum = sum(
        p[beam_width + 1 : beam_width + 2] * jnp.exp(p[beam_width : beam_width + 1] - cmax)
        for p in parts
    )
    logprob = sum(p[0:beam_width] for p in parts) - (cmax + jnp.log(csum))
    logprob_ref[...] = logprob[:, 0:rows]

    sources = [lax.rem(chip + offset, chips) for offset in range(1, chips)]
    for g in sources:
        push(stat_send.at[0], stat_recv.at[g], stat_send_sem.at[0], stat_recv_sem.at[g], sibling).wait_recv()
    stats = [stat_recv[g] for g in sources]
    overall = functools.reduce(jnp.maximum, [t[0:1] for t in stats], own_high)
    own_share = jnp.exp(own_high - overall)
    shares = [jnp.exp(t[0:1] - overall) for t in stats]
    whole = own_amount * own_share + sum(f * t[1:2] for f, t in zip(shares, stats))
    merged = own_both * to_column(own_share / whole)
    for g, share, stat in zip(sources, shares, stats):
        push(code_send.at[0], code_recv.at[g], code_send_sem.at[0], code_recv_sem.at[g], sibling).wait_recv()
        merged = merged + code_recv[g].astype(jnp.int32).astype(f32) * to_column(
            share * stat[2:3] / whole
        )
    readout_ref[...] = merged.astype(jnp.bfloat16)

    for copy in sends + centroid_copies + near_copies + result_copies:
        copy.wait_send()


def store_kernel(readout_ref, logprob_ref, readout_out, logprob_out, sems):
    copies = [
        pltpu.make_async_copy(readout_ref, readout_out, sems.at[0]),
        pltpu.make_async_copy(logprob_ref, logprob_out, sems.at[1]),
    ]
    for copy in copies:
        copy.start()
    for copy in copies:
        copy.wait()


def fused(queries, centroids, leaves, beam):
    groups = lax.axis_size("cluster")
    rows, width = queries.shape
    clusters = centroids.shape[0]
    total, beam_width = beam.shape
    capacity = 2 * total * beam_width // (clusters * groups)
    if rows % 16 or capacity % 16 or groups % 2 or groups > 16 or rows > LANES or beam_width != 8:
        return per_device(queries, centroids, leaves, beam)
    vmem = pl.BlockSpec(memory_space=pltpu.VMEM)
    hbm = pl.BlockSpec(memory_space=pltpu.HBM)
    dma = pltpu.SemaphoreType.DMA
    peers = groups - 1
    chips = groups // 2
    readout, logprob = pl.pallas_call(
        functools.partial(fused_kernel, groups, capacity),
        out_shape=(
            jax.ShapeDtypeStruct((rows, width), jnp.bfloat16),
            jax.ShapeDtypeStruct((beam_width, rows), jnp.float32),
        ),
        in_specs=[hbm, hbm, hbm, hbm],
        out_specs=(vmem, vmem),
        scratch_shapes=[
            pltpu.VMEM((groups, rows, width), jnp.bfloat16),
            pltpu.VMEM(centroids.shape, jnp.bfloat16),
            pltpu.VMEM((beam_width, total), jnp.int32),
            pltpu.VMEM(leaves.shape, jnp.bfloat16),
            pltpu.VMEM((groups, beam_width + 8, LANES), jnp.float32),
            pltpu.VMEM((groups, beam_width + 8, LANES), jnp.float32),
            pltpu.VMEM((2, chips, rows, width), jnp.float32),
            pltpu.VMEM((chips, rows, width), jnp.float32),
            pltpu.VMEM((2, chips, 8, LANES), jnp.float32),
            pltpu.VMEM((chips, 8, LANES), jnp.float32),
            pltpu.VMEM((chips, 8, LANES), jnp.float32),
            pltpu.VMEM((chips, 8, LANES), jnp.float32),
            pltpu.VMEM((chips, rows, width), jnp.int16),
            pltpu.VMEM((chips, rows, width), jnp.int16),
            dma((clusters,)),
            dma((3,)),
            dma((groups,)),
            dma((groups,)),
            dma((peers,)),
            dma((groups,)),
            dma((chips + 1,)),
            dma((chips + 1,)),
            dma((chips,)),
            dma((chips,)),
            dma((chips,)),
            dma((chips,)),
        ],
        compiler_params=pltpu.CompilerParams(
            collective_id=0, has_side_effects=True, vmem_limit_bytes=64 * 1024 * 1024
        ),
    )(queries, centroids, leaves, beam.T)
    readout, logprob = pl.pallas_call(
        store_kernel,
        out_shape=(
            jax.ShapeDtypeStruct(readout.shape, readout.dtype),
            jax.ShapeDtypeStruct(logprob.shape, logprob.dtype),
        ),
        in_specs=[hbm, hbm],
        out_specs=(hbm, hbm),
        scratch_shapes=[dma((2,))],
        compiler_params=pltpu.CompilerParams(vmem_limit_bytes=64 * 1024 * 1024),
    )(readout, logprob)
    return readout, logprob.T


def solution(mesh):
    return jax.shard_map(
        fused,
        mesh=mesh,
        in_specs=(
            P(("query", "cluster"), None),
            P("cluster", None),
            P("cluster", None, None),
            P("query", None),
        ),
        out_specs=(P(("query", "cluster"), None), P(("query", "cluster"), None)),
        check_vma=False,
    )
```

```python
import functools
import math

import jax
import jax.numpy as jnp
from jax import lax
from jax.experimental import pallas as pl
from jax.experimental.pallas import tpu as pltpu
from jax.sharding import PartitionSpec as P

floor_value = -1e30


def merged_2(part, axis, combine):
    gathered = jax.tree.map(lambda a: lax.all_gather(a, axis), part)

    def take(source):
        return jax.tree.map(lambda a: lax.dynamic_index_in_dim(a, source, 0, False), gathered)

    return lax.fori_loop(
        1, lax.axis_size(axis), lambda source, state: combine(state, take(source)), take(0)
    )


def combine_states(first, second):
    cmax_one, csum_one, beam_one, lmax_one, lsum_one, accum_one = first
    cmax_two, csum_two, beam_two, lmax_two, lsum_two, accum_two = second
    cmax_new = jnp.maximum(cmax_one, cmax_two)
    csum_new = csum_one * jnp.exp(cmax_one - cmax_new) + csum_two * jnp.exp(cmax_two - cmax_new)
    lmax_new = jnp.maximum(lmax_one, lmax_two)
    factor_one = jnp.exp(lmax_one - lmax_new)
    factor_two = jnp.exp(lmax_two - lmax_new)
    lsum_new = lsum_one * factor_one + lsum_two * factor_two
    accum_new = accum_one * factor_one[:, None] + accum_two * factor_two[:, None]
    return (cmax_new, csum_new, beam_one + beam_two, lmax_new, lsum_new, accum_new)


def per_device(queries, centroids, leaves, beam):
    groups = lax.axis_size("cluster")
    query_block = lax.all_gather(queries, "cluster", axis=0, tiled=True)
    query_count, model_width = query_block.shape
    cluster_count, leaf_count, unused_width = leaves.shape
    beam_width = beam.shape[1]
    score_scale = 1.0 / math.sqrt(model_width)
    first_cluster = lax.axis_index("cluster") * cluster_count
    cscore = jnp.dot(query_block, centroids.T, preferred_element_type=jnp.float32) * score_scale
    cmax_part = jnp.max(cscore, axis=1)
    csum_part = jnp.sum(jnp.exp(cscore - cmax_part[:, None]), axis=1)
    owned = first_cluster + jnp.arange(cluster_count, dtype=jnp.int32)
    matches = beam[:, :, None] == owned[None, None, :]
    beam_part = jnp.sum(jnp.where(matches, cscore[:, None, :], 0.0), axis=2)
    membership = jnp.any(matches, axis=1).astype(jnp.int32)
    slot_index = jnp.cumsum(membership, axis=0) - 1
    capacity = max(4, 2 * query_count * beam_width // (cluster_count * groups))
    positions = jnp.arange(capacity, dtype=jnp.int32)
    dispatch = (membership.T[:, None, :] == 1) & (
        slot_index.T[:, None, :] == positions[None, :, None]
    )
    picked = jnp.einsum(
        "csq,qd->csd",
        dispatch.astype(jnp.bfloat16),
        query_block,
        preferred_element_type=jnp.float32,
    ).astype(jnp.bfloat16)
    slot_centroid = jnp.sum(jnp.where(dispatch, cscore.T[:, None, :], 0.0), axis=2)
    logits = (
        jnp.einsum("csd,cjd->csj", picked, leaves, preferred_element_type=jnp.float32) * score_scale
    )
    logits = logits + slot_centroid[:, :, None]
    slot_max = jnp.max(logits, axis=2)
    weights = jnp.exp(logits - slot_max[:, :, None])
    slot_sum = jnp.sum(weights, axis=2)
    slot_accum = jnp.einsum(
        "csj,cjd->csd", weights.astype(jnp.bfloat16), leaves, preferred_element_type=jnp.float32
    )
    slot_total = cluster_count * capacity
    dispatch_flat = dispatch.reshape(slot_total, query_count)
    slot_max_flat = slot_max.reshape(slot_total)
    masked_max = jnp.where(dispatch_flat, slot_max_flat[:, None], floor_value)
    lmax_part = jnp.max(masked_max, axis=0)
    exponent = jnp.where(dispatch_flat, slot_max_flat[:, None] - lmax_part[None, :], 0.0)
    factors = jnp.where(dispatch_flat, jnp.exp(exponent), 0.0)
    lsum_part = jnp.sum(factors * slot_sum.reshape(slot_total)[:, None], axis=0)
    accum_part = jnp.dot(
        factors.T,
        slot_accum.reshape(slot_total, model_width),
        precision=lax.Precision.HIGHEST,
        preferred_element_type=jnp.float32,
    )
    state = (cmax_part, csum_part, beam_part, lmax_part, lsum_part, accum_part)
    row_count = query_count // groups
    merged = merged_2(state, "cluster", combine_states)
    row_start = lax.axis_index("cluster") * row_count
    own = tuple((lax.dynamic_slice_in_dim(member, row_start, row_count, 0) for member in merged))
    cmax_own, csum_own, beam_own, lmax_own, lsum_own, accum_own = own
    lse = cmax_own + jnp.log(csum_own)
    beam_logprob = beam_own - lse[:, None]
    readout = (accum_own / lsum_own[:, None]).astype(jnp.bfloat16)
    return (readout, beam_logprob)


MESH = pl.DeviceIdType.MESH
CODE_MAX = 32767.0
LANES = 128


def fused_kernel(
    groups,
    capacity,
    q_ref,
    cent_ref,
    leaves_ref,
    beam_ref,
    readout_ref,
    logprob_ref,
    block,
    cent_buf,
    beam_buf,
    leaf_buf,
    weight_buf,
    centroid_send,
    centroid_recv,
    held_buf,
    near_recv,
    level_buf,
    near_level,
    stat_send,
    stat_recv,
    code_send,
    code_recv,
    leaf_sem,
    own_sem,
    q_send_sem,
    q_recv_sem,
    centroid_send_sem,
    centroid_recv_sem,
    near_send_sem,
    near_recv_sem,
    stat_send_sem,
    stat_recv_sem,
    code_send_sem,
    code_recv_sem,
):
    rows, width = q_ref.shape
    clusters = cent_ref.shape[0]
    total = groups * rows
    beam_width = beam_ref.shape[0]
    chips = groups // 2
    half = width // 2
    score_scale = 1.0 / math.sqrt(width)
    f32 = jnp.float32
    me = lax.axis_index("cluster")
    chip, core = me // 2, me % 2
    sibling = chip * 2 + (1 - core)
    first = me * clusters

    def peer_at(offset, side):
        return lax.rem(chip + offset, chips) * 2 + side

    peers = [peer_at(o, s) for o in range(1, chips) for s in (core, 1 - core)] + [sibling]

    def signal_peers():
        barrier = pltpu.get_barrier_semaphore()
        for peer in peers:
            pl.semaphore_signal(barrier, inc=1, device_id={"cluster": peer}, device_id_type=MESH)
        pl.semaphore_wait(barrier, len(peers))

    own_copies = [
        pltpu.make_async_copy(q_ref, block.at[me], own_sem.at[0]),
        pltpu.make_async_copy(beam_ref, beam_buf, own_sem.at[1]),
        pltpu.make_async_copy(cent_ref, cent_buf, own_sem.at[2]),
    ]
    leaf_copies = [
        pltpu.make_async_copy(leaves_ref.at[c], leaf_buf.at[c], leaf_sem.at[c])
        for c in range(clusters)
    ]
    for copy in own_copies + leaf_copies:
        copy.start()
    signal_peers()

    def push(src, dst, send_sem, recv_sem, peer):
        return pltpu.make_async_remote_copy(
            src_ref=src,
            dst_ref=dst,
            send_sem=send_sem,
            recv_sem=recv_sem,
            device_id={"cluster": peer},
            device_id_type=MESH,
        )

    own_copies[0].wait()
    mine = block.at[me]
    sends = []
    for number, offset in enumerate(range(1, chips)):
        peer = peer_at(offset, core)
        sends.append(push(mine, mine, q_send_sem.at[number], q_recv_sem.at[me], peer))
    sends.append(push(mine, mine, q_send_sem.at[chips - 1], q_recv_sem.at[me], sibling))
    for copy in sends:
        copy.start()

    own_copies[1].wait()
    beams = beam_buf[...]
    members = jnp.concatenate(
        [
            jnp.max((beams == first + c).astype(f32), axis=0, keepdims=True)
            for c in range(clusters)
        ],
        axis=0,
    )
    upper = (
        lax.broadcasted_iota(jnp.int32, (total, total), 0)
        <= lax.broadcasted_iota(jnp.int32, (total, total), 1)
    ).astype(jnp.bfloat16)
    padded = jnp.concatenate([members, jnp.zeros((LANES - clusters, total), f32)], axis=0)
    counts = jnp.dot(padded.astype(jnp.bfloat16), upper, preferred_element_type=f32)
    slots = jnp.where(padded > 0.0, counts, 0.0)
    slot_number = lax.broadcasted_iota(jnp.int32, (capacity, total), 0).astype(f32) + 1.0
    dispatch = jnp.concatenate(
        [(slots[c : c + 1, :] == slot_number).astype(f32) for c in range(clusters)], axis=0
    )
    slot_total = clusters * capacity
    slots_down = slots.T
    slot_across = lax.broadcasted_iota(jnp.int32, (total, slot_total), 1)
    wanted = jnp.concatenate(
        [jnp.broadcast_to(slots_down[:, c : c + 1], (total, capacity)) for c in range(clusters)],
        axis=1,
    )
    collect = (wanted == (slot_across % capacity).astype(f32) + 1.0).astype(jnp.bfloat16)

    def arrival(origin):
        return push(block.at[origin], block.at[origin], q_send_sem.at[0], q_recv_sem.at[origin], sibling)

    for offset in range(1, chips):
        origin = peer_at(chips - offset, core)
        arrival(origin).wait_recv()
        relay = push(
            block.at[origin],
            block.at[origin],
            q_send_sem.at[chips - 1 + offset],
            q_recv_sem.at[origin],
            sibling,
        )
        relay.start()
        sends.append(relay)
    arrival(sibling).wait_recv()
    for offset in range(1, chips):
        arrival(peer_at(chips - offset, 1 - core)).wait_recv()
    own_copies[2].wait()

    queries = block[...].reshape(total, width)
    cent = jnp.concatenate(
        [cent_buf[...], jnp.zeros((LANES - clusters, width), cent_buf.dtype)], axis=0
    )
    nt = (((1,), (1,)), ((), ()))
    cscore = lax.dot_general(cent, queries, nt, preferred_element_type=f32)[0:clusters]
    cscore = cscore * score_scale
    part_max = jnp.max(cscore, axis=0, keepdims=True)
    part_sum = jnp.sum(jnp.exp(cscore - part_max), axis=0, keepdims=True)
    picks = sum(
        jnp.where(beams == first + c, cscore[c : c + 1, :], 0.0) for c in range(clusters)
    )
    for g in range(groups):
        lanes = slice(g * rows, (g + 1) * rows)
        centroid_send[g, 0:beam_width, 0:rows] = picks[:, lanes]
        centroid_send[g, beam_width : beam_width + 1, 0:rows] = part_max[:, lanes]
        centroid_send[g, beam_width + 1 : beam_width + 2, 0:rows] = part_sum[:, lanes]
    centroid_copies = [
        push(
            centroid_send.at[peer],
            centroid_recv.at[me],
            centroid_send_sem.at[number],
            centroid_recv_sem.at[me],
            peer,
        )
        for number, peer in enumerate(peers)
    ]
    for copy in centroid_copies:
        copy.start()

    picked = jnp.dot(
        dispatch.astype(jnp.bfloat16), queries, preferred_element_type=f32
    ).astype(jnp.bfloat16)
    lane = lax.broadcasted_iota(jnp.int32, (slot_total, LANES), 1)
    owner = lax.broadcasted_iota(jnp.int32, (slot_total, LANES), 0) // capacity
    slot_scores = lax.dot_general(picked, cent, nt, preferred_element_type=f32) * score_scale
    slot_centroid = jnp.sum(jnp.where(lane == owner, slot_scores, 0.0), axis=1, keepdims=True)
    for copy in leaf_copies:
        copy.wait()

    def scores(c):
        return lax.dot_general(
            picked[c * capacity : (c + 1) * capacity],
            leaf_buf[c],
            nt,
            preferred_element_type=f32,
        )

    def weigh(c, h):
        return jnp.dot(
            weight_buf[c],
            leaf_buf[c, :, h * half : (h + 1) * half],
            preferred_element_type=f32,
        )

    peaks, masses, sums = [], [], []
    current = scores(0)
    for c in range(clusters):
        upcoming = scores(c + 1) if c + 1 < clusters else None
        peak = jnp.max(current, axis=1, keepdims=True)
        weights = jnp.exp((current - peak) * score_scale)
        masses.append(jnp.sum(weights, axis=1, keepdims=True))
        peaks.append(peak)
        weight_buf[c] = weights.astype(jnp.bfloat16)
        sums.append(weigh(c, 0))
        current = upcoming
    level = jnp.concatenate(peaks, axis=0) * score_scale + slot_centroid
    mass = jnp.concatenate(masses, axis=0)

    used = dispatch > 0.0
    top = jnp.max(jnp.where(used, level, floor_value), axis=0, keepdims=True)
    slot_top = jnp.max(jnp.where(used, top, floor_value), axis=1, keepdims=True)
    filled = jnp.max(dispatch, axis=1, keepdims=True) > 0.0
    gain = jnp.where(filled, jnp.exp(jnp.where(filled, level - slot_top, 0.0)), 0.0)
    denom = jnp.sum(jnp.where(used, mass * gain, 0.0), axis=0, keepdims=True)
    for g in range(groups):
        lanes = slice(g * rows, (g + 1) * rows)
        level_buf[g % 2, g // 2, 0:1, 0:rows] = top[:, lanes]
        level_buf[g % 2, g // 2, 1:2, 0:rows] = denom[:, lanes]
    order = [2, 1, 3, 0] if chips == 4 else list(range(1, chips)) + [0]
    level_copy = push(
        level_buf.at[1 - core],
        near_level,
        near_send_sem.at[0, chips],
        near_recv_sem.at[0, chips],
        sibling,
    )
    level_copy.start()
    near_copies = [level_copy]

    def near_copy(h, offset):
        g = lax.rem(chip + offset, chips)
        return push(
            held_buf.at[h, 1 - core, g],
            near_recv.at[h, g],
            near_send_sem.at[h, offset],
            near_recv_sem.at[h, g],
            sibling,
        )

    def share_half(h, sums):
        scaled = jnp.concatenate(sums, axis=0) * gain
        coarse = scaled.astype(jnp.bfloat16)
        fine = (scaled - coarse.astype(f32)).astype(jnp.bfloat16)
        held = jnp.dot(collect, coarse, preferred_element_type=f32) + jnp.dot(
            collect, fine, preferred_element_type=f32
        )
        for g in range(groups):
            held_buf[h, g % 2, g // 2] = held[g * rows : (g + 1) * rows]
        for offset in order:
            near_copies.append(near_copy(h, offset))
            near_copies[-1].start()

    diagonal = lax.broadcasted_iota(jnp.int32, (rows, LANES), 0) == lax.broadcasted_iota(
        jnp.int32, (rows, LANES), 1
    )

    def to_column(row):
        return jnp.sum(jnp.where(diagonal, row, 0.0), axis=1, keepdims=True)

    def to_row(column):
        return jnp.sum(jnp.where(diagonal, column, 0.0), axis=0, keepdims=True)

    result_copies = []

    def chip_levels():
        level_copy.wait_recv()
        found = []
        for offset in order:
            g = lax.rem(chip + offset, chips)
            here, near = level_buf[core, g], near_level[g]
            high = jnp.maximum(here[0:1], near[0:1])
            here_gain, near_gain = jnp.exp(here[0:1] - high), jnp.exp(near[0:1] - high)
            amount = here[1:2] * here_gain + near[1:2] * near_gain
            found.append((high, amount, to_column(here_gain), to_column(near_gain)))
        return found

    def merge_half(h, levels):
        for number, offset in enumerate(order):
            g = lax.rem(chip + offset, chips)
            high, amount, here_gain, near_gain = levels[number]
            near_copy(h, offset).wait_recv()
            both = held_buf[h, core, g] * here_gain + near_recv[h, g] * near_gain
            if offset == 0:
                return both
            largest = jnp.maximum(jnp.max(jnp.abs(both), axis=1, keepdims=True), 1e-30)
            code_send[h, number] = (
                jnp.round(both * (CODE_MAX / largest)).astype(jnp.int32).astype(jnp.int16)
            )
            stat_send[h, number, 0:1] = high
            stat_send[h, number, 1:2] = amount
            stat_send[h, number, 2:3] = to_row(largest * (1.0 / CODE_MAX))
            peer = g * 2 + core
            for source, target, send_sem, recv_sem in (
                (stat_send, stat_recv, stat_send_sem, stat_recv_sem),
                (code_send, code_recv, code_send_sem, code_recv_sem),
            ):
                copy = push(
                    source.at[h, number],
                    target.at[h, chip],
                    send_sem.at[h, number],
                    recv_sem.at[h, chip],
                    peer,
                )
                copy.start()
                result_copies.append(copy)

    share_half(0, sums)
    sums_high = [weigh(c, 1) for c in range(clusters // 2)]
    levels = chip_levels()
    own_low = merge_half(0, levels)
    sums_high += [weigh(c, 1) for c in range(clusters // 2, clusters)]
    share_half(1, sums_high)
    own_high_half = merge_half(1, levels)
    own_top, own_amount = levels[-1][0], levels[-1][1]

    for number, peer in enumerate(peers):
        push(
            centroid_send.at[peer],
            centroid_recv.at[peer],
            centroid_send_sem.at[number],
            centroid_recv_sem.at[peer],
            peer,
        ).wait_recv()
    centroid_recv[me] = centroid_send[me]
    parts = [centroid_recv[g] for g in range(groups)]
    cmax = functools.reduce(jnp.maximum, [p[beam_width : beam_width + 1] for p in parts])
    csum = sum(
        p[beam_width + 1 : beam_width + 2] * jnp.exp(p[beam_width : beam_width + 1] - cmax)
        for p in parts
    )
    logprob = sum(p[0:beam_width] for p in parts) - (cmax + jnp.log(csum))
    logprob_ref[...] = logprob[:, 0:rows]

    sources = [lax.rem(chip + offset, chips) for offset in range(1, chips)]
    own_share = whole = None
    for h, own in enumerate((own_low, own_high_half)):
        for g in sources:
            push(
                stat_send.at[h, 0],
                stat_recv.at[h, g],
                stat_send_sem.at[h, 0],
                stat_recv_sem.at[h, g],
                sibling,
            ).wait_recv()
        stats = [stat_recv[h, g] for g in sources]
        if h == 0:
            overall = functools.reduce(jnp.maximum, [t[0:1] for t in stats], own_top)
            own_share = jnp.exp(own_top - overall)
            shares = [jnp.exp(t[0:1] - overall) for t in stats]
            whole = own_amount * own_share + sum(f * t[1:2] for f, t in zip(shares, stats))
        merged = own * to_column(own_share / whole)
        for g, share, stat in zip(sources, shares, stats):
            push(
                code_send.at[h, 0],
                code_recv.at[h, g],
                code_send_sem.at[h, 0],
                code_recv_sem.at[h, g],
                sibling,
            ).wait_recv()
            merged = merged + code_recv[h, g].astype(jnp.int32).astype(f32) * to_column(
                share * stat[2:3] / whole
            )
        readout_ref[:, h * half : (h + 1) * half] = merged.astype(jnp.bfloat16)

    for copy in sends + centroid_copies + near_copies + result_copies:
        copy.wait_send()


def store_kernel(readout_ref, logprob_ref, readout_out, logprob_out, sems):
    copies = [
        pltpu.make_async_copy(readout_ref, readout_out, sems.at[0]),
        pltpu.make_async_copy(logprob_ref, logprob_out, sems.at[1]),
    ]
    for copy in copies:
        copy.start()
    for copy in copies:
        copy.wait()


def fused(queries, centroids, leaves, beam):
    groups = lax.axis_size("cluster")
    rows, width = queries.shape
    clusters = centroids.shape[0]
    total, beam_width = beam.shape
    capacity = 2 * total * beam_width // (clusters * groups)
    if rows % 16 or capacity % 16 or groups % 2 or groups > 16 or rows > LANES or beam_width != 8 or width % 256:
        return per_device(queries, centroids, leaves, beam)
    vmem = pl.BlockSpec(memory_space=pltpu.VMEM)
    hbm = pl.BlockSpec(memory_space=pltpu.HBM)
    dma = pltpu.SemaphoreType.DMA
    peers = groups - 1
    chips = groups // 2
    half = width // 2
    readout, logprob = pl.pallas_call(
        functools.partial(fused_kernel, groups, capacity),
        out_shape=(
            jax.ShapeDtypeStruct((rows, width), jnp.bfloat16),
            jax.ShapeDtypeStruct((beam_width, rows), jnp.float32),
        ),
        in_specs=[hbm, hbm, hbm, hbm],
        out_specs=(vmem, vmem),
        scratch_shapes=[
            pltpu.VMEM((groups, rows, width), jnp.bfloat16),
            pltpu.VMEM(centroids.shape, jnp.bfloat16),
            pltpu.VMEM((beam_width, total), jnp.int32),
            pltpu.VMEM(leaves.shape, jnp.bfloat16),
            pltpu.VMEM((clusters, capacity, leaves.shape[1]), jnp.bfloat16),
            pltpu.VMEM((groups, beam_width + 8, LANES), jnp.float32),
            pltpu.VMEM((groups, beam_width + 8, LANES), jnp.float32),
            pltpu.VMEM((2, 2, chips, rows, half), jnp.float32),
            pltpu.VMEM((2, chips, rows, half), jnp.float32),
            pltpu.VMEM((2, chips, 8, LANES), jnp.float32),
            pltpu.VMEM((chips, 8, LANES), jnp.float32),
            pltpu.VMEM((2, chips, 8, LANES), jnp.float32),
            pltpu.VMEM((2, chips, 8, LANES), jnp.float32),
            pltpu.VMEM((2, chips, rows, half), jnp.int16),
            pltpu.VMEM((2, chips, rows, half), jnp.int16),
            dma((clusters,)),
            dma((3,)),
            dma((groups,)),
            dma((groups,)),
            dma((peers,)),
            dma((groups,)),
            dma((2, chips + 1)),
            dma((2, chips + 1)),
            dma((2, chips)),
            dma((2, chips)),
            dma((2, chips)),
            dma((2, chips)),
        ],
        compiler_params=pltpu.CompilerParams(
            collective_id=0, has_side_effects=True, vmem_limit_bytes=64 * 1024 * 1024
        ),
    )(queries, centroids, leaves, beam.T)
    readout, logprob = pl.pallas_call(
        store_kernel,
        out_shape=(
            jax.ShapeDtypeStruct(readout.shape, readout.dtype),
            jax.ShapeDtypeStruct(logprob.shape, logprob.dtype),
        ),
        in_specs=[hbm, hbm],
        out_specs=(hbm, hbm),
        scratch_shapes=[dma((2,))],
        compiler_params=pltpu.CompilerParams(vmem_limit_bytes=64 * 1024 * 1024),
    )(readout, logprob)
    return readout, logprob.T


def solution(mesh):
    return jax.shard_map(
        fused,
        mesh=mesh,
        in_specs=(
            P(("query", "cluster"), None),
            P("cluster", None),
            P("cluster", None, None),
            P("query", None),
        ),
        out_specs=(P(("query", "cluster"), None), P(("query", "cluster"), None)),
        check_vma=False,
    )
```
